32 devices in a mesh: groups: 2 (over x), expert: 16 (over z, y, core).
Axes of the slice: x: 2, y: 2, z: 4, core: 2. Of those that a mesh axis runs over, the one named last changes fastest.
Arguments:
- tokens: bfloat16 [512, 2048], P(('groups', 'expert')), parts along dimension 0, may hold values from -6 to 6
- depths: int32 [512], P(('groups', 'expert')), parts along dimension 0, may hold values from 1 to 2
- routes: int32 [2, 512, 8], P(None, ('groups', 'expert')), parts along dimension 1, may hold values from 0 to 15, all different within a row; in each aligned block of 16 rows (0 to 15, 16 to 31, ..., all dimensions but the last counted through in order) at most 16 rows name the same one
- norm_gain: bfloat16 [2048], replicated, may hold values from 0.099609375 to 1.8984375
- router: bfloat16 [2048, 16], replicated, may hold values from -0.125 to 0.125
- w_gate: bfloat16 [16, 2048, 768], P('expert'), may hold values from -0.125 to 0.125
- w_up: bfloat16 [16, 2048, 768], P('expert'), may hold values from -0.125 to 0.125
- w_down: bfloat16 [16, 768, 2048], P('expert'), may hold values from -0.21875 to 0.21875
- replica_plan: int32 [16], replicated, may hold values from 0 to 15, as said below
- copy_choice: int32 [16, 16], P('expert'), may hold values from 0 to 15, as said below
Outputs:
- final_state: bfloat16 [512, 2048], P(('groups', 'expert')), parts along dimension 0
- copy_load: float32 [32, 4], P(('groups', 'expert')), parts along dimension 0
The draws below stay inside these ranges and needn't reach their ends.
There are 2 independent parts, one for each index of `groups`. The reference program is written for one: setup_inputs(seed, part) draws one part's arguments, and reference() takes and returns one part's arrays. A program takes and returns all parts, laid end to end along the dimension named above; an argument that names none is the same for every part. Nothing has to cross between parts.
Inputs may be any that keep to these rules, and one draw needn't show every extreme that they name: `routes`: in each pass the 8 experts of a row differ, and no expert is named by more than 16 rows of one device (an aligned block of 16 rows); some expert is named by exactly 16 rows in some blocks. replica_plan[d] is never d. copy_choice[s, e] is a device number.
All inputs are finite; a program needn't handle non-finite values.
Results may differ from the reference program's by a relative error of at most 0.0038.
The reference program's roundings to bfloat16 on the way count: a program that leaves them out, or rounds other values in their place, can miss the bound.
Values may be sent and summed in bfloat16 or wider, within the bound.
A program may use at most 64 MiB of HBM per device.

```python
import math
import jax
import jax.numpy as jnp
import numpy as np
from jax import lax

D = 2048
FF = 768
TOP = 8
ITERS = 2
TOK_DEV = 16
EXPERTS = 16
MOST = 16
TOKENS = 256
N_EXPERT = 16


def make_plan(key):
    hot_count = EXPERTS // 8
    order = jax.random.permutation(jax.random.fold_in(key, 11), EXPERTS).astype(jnp.int32)
    hot_list = order[:hot_count]
    choose = jax.random.randint(jax.random.fold_in(key, 12), (EXPERTS,), 0, hot_count)
    device_ids = jnp.arange(EXPERTS, dtype=jnp.int32)
    first = hot_list[choose]
    second = hot_list[(choose + 1) % hot_count]
    return jnp.where(first == device_ids, second, first).astype(jnp.int32)


def draw_replica_plan(key, part):
    return make_plan(key)


def draw_copy_choice(key, part):
    plan_table = make_plan(key)
    ident = jnp.arange(EXPERTS, dtype=jnp.int32)
    holds = (plan_table[None, :] == ident[:, None]).astype(jnp.int32)
    ranks = jnp.cumsum(holds, axis=1) * holds
    copies = 1 + jnp.sum(holds, axis=1)
    pick_copy = jax.random.randint(jax.random.fold_in(key, 13), (EXPERTS, EXPERTS), 0, copies[None, :])
    match = (ranks[None, :, :] == pick_copy[:, :, None]) & (holds[None, :, :] == 1)
    other = jnp.sum(jnp.where(match, ident[None, None, :], 0), axis=2)
    return jnp.where(pick_copy == 0, ident[None, :], other).astype(jnp.int32)


def plant(result, rng, low, largest):
    place = [jax.random.randint(jax.random.fold_in(rng, axis), (), 0, length) for axis, length in enumerate(result.shape)]
    main_axis = result.shape.index(max(result.shape))
    beside = place[:main_axis] + [(place[main_axis] + 1) % result.shape[main_axis]] + place[main_axis + 1:]
    return result.at[tuple(place)].set(low).at[tuple(beside)].set(largest)


def shard_levels(rng, extent, cuts, least, top_value):
    def one(dim, shards_of):
        heights = jax.random.uniform(jax.random.fold_in(jax.random.fold_in(rng, 6), dim), (shards_of,), jnp.float32, least / len(cuts), top_value / len(cuts))
        return jnp.repeat(jnp.exp(heights), extent[dim] // shards_of).reshape((-1,) + (1,) * (len(extent) - dim - 1))

    factor_of = one(*cuts[0])
    for cut in cuts[1:]:
        factor_of = factor_of * one(*cut)
    return factor_of


def shared_out(key, own, number, rows, number_of, top, most, slope):
    sequence = jax.random.permutation(key, number_of)
    packed, ordinary = portions_of(number_of, rows * top, most, slope, True), portions_of(number_of, rows * top, most, slope, False)
    places = jnp.arange(number_of)

    def named(lengths, offset_by):
        used = int((lengths > 0).sum())
        fixed = max(1, used // 4)
        shifted = fixed + (places - fixed + offset_by * (used - fixed)) % max(1, number_of - fixed)
        return jnp.zeros((number_of,), jnp.int32).at[sequence[jnp.where(places < fixed, places, shifted)]].set(jnp.asarray(lengths, jnp.int32))

    lengths = jnp.where(number % 4 == 0, named(packed, number // 4), named(ordinary, number - number // 4 - 1))
    mixed = jax.random.permutation(jax.random.fold_in(own, 3), number_of)
    giver, receiver = mixed[0:number_of // 2 * 2:2], mixed[1:number_of // 2 * 2:2]
    slack = jnp.minimum(lengths[giver] - 1, most - lengths[receiver]) // 2
    slack = jnp.where((giver == sequence[0]) | (receiver == sequence[0]) | (lengths[receiver] == 0), 0, jnp.maximum(slack, 0))
    shifted = jax.random.randint(jax.random.fold_in(own, 4), (number_of // 2,), 0, 1 << 20) % (slack + 1)
    lengths = lengths.at[giver].add(-shifted).at[receiver].add(shifted)
    labels = jnp.searchsorted(jnp.cumsum(lengths), jnp.arange(rows * top), side="right").astype(jnp.int32)
    listing = labels.reshape(top, rows).T
    listing = listing[jax.random.permutation(jax.random.fold_in(own, 1), rows)]
    offset_by = jax.random.randint(jax.random.fold_in(own, 2), (rows, 1), 0, top)
    return jnp.take_along_axis(listing, (jnp.arange(top)[None, :] + offset_by) % top, axis=1)


def portions_of(amount, total, limit, slope, full):
    portions = [(1 << 20) // math.isqrt(grade ** slope) + 1 for grade in range(1, amount + 1)]
    largest = limit if full else min(limit, max(-(-total // amount), total * portions[0] // sum(portions)))
    least = 1 if total - largest >= amount - 1 else 0
    given, spare = [largest] + [least] * (amount - 1), total - largest - least * (amount - 1)
    while spare > 0:
        movable = [i for i in range(1, amount) if given[i] < largest] or [i for i in range(1, amount) if given[i] < limit]
        mass, budget = sum([portions[i] for i in movable]), spare
        for i in movable:
            more = min(limit - given[i], max(1, budget * portions[i] // mass), spare)
            given[i] = given[i] + more
            spare = spare - more
    return np.array(given)


def scatter_about(key, dims, scale, limit, split=(), held_as=jnp.bfloat16):
    array = jax.random.normal(key, dims, jnp.float32) * scale
    if len(split) > 0:
        array = shard_levels(key, dims, split, -0.22, 0.18) * array
    return jnp.clip(array, min=-limit, max=limit).astype(held_as)


def setup_inputs(seed: int = 0, part: int = 0) -> dict:
    key_of = jax.random.split(jax.random.key(seed), 11)
    part_splits = jax.random.split(jax.random.fold_in(key_of[10], part), 11)
    tokens = scatter_about(part_splits[0], (TOKENS, D), 1.0, 6.0, ((0, 16),))
    depths = plant(jax.random.randint(part_splits[1], (TOKENS,), 1, 3), jax.random.fold_in(part_splits[1], 1), 1, 2).astype(jnp.int32)
    routes_keys = jax.random.split(jax.random.fold_in(part_splits[2], 1), ITERS * TOKENS // TOK_DEV)
    routes_turns = jax.random.permutation(jax.random.fold_in(part_splits[2], 3), ITERS * TOKENS // TOK_DEV)
    routes = jax.vmap(lambda own, number: shared_out(jax.random.fold_in(part_splits[2], 2), own, number, TOK_DEV, EXPERTS, TOP, MOST, 2))(routes_keys, routes_turns).reshape((ITERS, TOKENS, TOP))
    norm_gain = jnp.clip(1.0 + 0.18 * jax.random.normal(key_of[3], (D,), jnp.float32), 0.099609375, 1.8984375).astype(jnp.bfloat16)
    router = scatter_about(key_of[4], (D, EXPERTS), D ** -0.5, 0.125)
    w_gate = scatter_about(key_of[5], (EXPERTS, D, FF), D ** -0.5, 0.125, ((0, 16),))
    w_up = scatter_about(key_of[6], (EXPERTS, D, FF), D ** -0.5, 0.125, ((0, 16),))
    w_down = scatter_about(key_of[7], (EXPERTS, FF, D), FF ** -0.5, 0.21875, ((0, 16),))
    replica_plan = draw_replica_plan(jax.random.fold_in(key_of[10], 71), part)
    copy_choice = draw_copy_choice(jax.random.fold_in(key_of[10], 71), part)
    return dict(tokens=tokens, depths=depths, routes=routes, norm_gain=norm_gain, router=router, w_gate=w_gate, w_up=w_up, w_down=w_down, replica_plan=replica_plan, copy_choice=copy_choice)


def expert_block(pieces):
    rows_in, gate_w, up_w, down_w = pieces
    highest = lax.Precision.HIGHEST
    gate_val = jnp.dot(rows_in.astype(jnp.float32), gate_w.astype(jnp.float32), precision=highest)
    up_val = jnp.dot(rows_in.astype(jnp.float32), up_w.astype(jnp.float32), precision=highest)
    hidden = (jax.nn.silu(gate_val) * up_val).astype(jnp.bfloat16)
    return jnp.dot(hidden.astype(jnp.float32), down_w.astype(jnp.float32), precision=highest).astype(jnp.bfloat16)

def reference(tokens, depths, routes, norm_gain, router, w_gate, w_up, w_down, replica_plan, copy_choice):
    highest = lax.Precision.HIGHEST
    capacity = N_EXPERT * MOST
    state = tokens
    row_ids = jnp.arange(TOKENS, dtype=jnp.int32)
    source = row_ids // TOK_DEV
    expert_ids = jnp.arange(EXPERTS, dtype=jnp.int32)
    pair_rows = jnp.broadcast_to(row_ids[:, None], (TOKENS, TOP)).reshape(-1)
    loads = []
    for layer_step in range(ITERS):
        state32 = state.astype(jnp.float32)
        scale = lax.rsqrt(lax.optimization_barrier(jnp.mean(state32 * state32, axis=1, keepdims=True)) + 1e-06)
        normed = (state32 * scale * norm_gain.astype(jnp.float32)).astype(jnp.bfloat16)
        logits = jnp.dot(normed, router, preferred_element_type=jnp.float32)
        chosen = routes[layer_step]
        picked = jnp.take_along_axis(logits, chosen, axis=1)
        sigmas = jax.nn.sigmoid(picked)
        gates = sigmas / lax.optimization_barrier(jnp.sum(sigmas, axis=1, keepdims=True))
        active = depths > layer_step
        onehot = (chosen[:, :, None] == expert_ids).astype(jnp.int32)
        ranks = jnp.cumsum(onehot.reshape(N_EXPERT, TOK_DEV * TOP, EXPERTS), axis=1).reshape(TOKENS, TOP, EXPERTS)
        position = lax.optimization_barrier(jnp.sum(ranks * onehot, axis=2)) - 1
        slot_index = (chosen * capacity + source[:, None] * MOST + position).reshape(-1).astype(jnp.int32)
        table = jnp.full((EXPERTS * capacity,), TOKENS, jnp.int32).at[slot_index].set(pair_rows)
        padded = jnp.concatenate([normed, jnp.zeros((1, D), jnp.bfloat16)], axis=0)

        def one_expert(pieces):
            index_rows, gate_w, up_w, down_w = pieces
            return expert_block((padded[index_rows], gate_w, up_w, down_w))
        outputs = lax.map(one_expert, (table.reshape(EXPERTS, capacity), w_gate, w_up, w_down))
        pair_out = outputs.reshape(EXPERTS * capacity, D)[slot_index].reshape(TOKENS, TOP, D)
        weights = gates * active[:, None].astype(jnp.float32)
        delta = jnp.einsum('rk,rkd->rd', weights, pair_out.astype(jnp.float32), precision=highest)
        state = (state32 + delta).astype(jnp.bfloat16)
        wanted = copy_choice[source[:, None], chosen]
        valid = (replica_plan[wanted] == chosen) & (wanted != chosen)
        target = jnp.where(valid, wanted, chosen).astype(jnp.int32)
        slot_bit = valid.astype(jnp.int32)
        bucket = (target * 2 + slot_bit).reshape(-1)
        live = jnp.broadcast_to(active[:, None], (TOKENS, TOP)).reshape(-1).astype(jnp.float32)
        counts = jax.ops.segment_sum(live, bucket, num_segments=2 * EXPERTS)
        loads.append(counts.reshape(EXPERTS, 2))
    copy_load = jnp.concatenate(loads, axis=1) / float(TOK_DEV * TOP)
    return (state, copy_load)
```

```python
import functools

import jax
import jax.numpy as jnp
from jax import lax
from jax.experimental import pallas as pl
from jax.experimental.pallas import tpu as pltpu
from jax.sharding import PartitionSpec as P

LANES = 128
FLAG = 32
LOADS = 48
CORES, CHIPS_Y, CHIPS_Z = 2, 2, 4
FUSED_DEVICES = CORES * CHIPS_Y * CHIPS_Z
CHUNKS = 4
TILE = 256


def fused_kernel(
    tokens, depths, routes, gain, router, gate_hbm, up_hbm, down_hbm, plan, choice,
    out, load,
    w_gate, w_up, w_down, state, counts, rows_all, hidden, gate_col,
    part, from_core, for_y, from_y, for_z, from_z,
    weight_sem, gather_send, gather_recv, core_send, core_recv, y_send, y_recv, z_send, z_recv,
):
    me = lax.axis_index("expert")
    core = me % CORES
    y = (me // CORES) % CHIPS_Y
    z = me // (CORES * CHIPS_Y)
    other_core, other_y = 1 - core, 1 - y
    other_z = (z + 1 - 2 * (z % 2), (z + 2) % CHIPS_Z, CHIPS_Z - 1 - z)

    def device(at_z, at_y, at_core):
        return {"expert": (at_z * CHIPS_Y + at_y) * CORES + at_core}

    def slot(at_core, at_y, at_z):
        return (at_core * CHIPS_Y + at_y) * CHIPS_Z + at_z

    sibling = device(z, y, other_core)
    across = device(z, other_y, core)
    along = [device(at, y, core) for at in other_z]

    iter_count, row_count, top_count = routes.shape
    width = tokens.shape[1]
    hidden_width = w_gate.shape[1]
    all_rows = FUSED_DEVICES * row_count
    chunk = width // CHUNKS
    half = CHIPS_Y * CHIPS_Z

    weights = [
        pltpu.make_async_copy(src.at[0], dst, weight_sem.at[i])
        for i, (src, dst) in enumerate(((gate_hbm, w_gate), (up_hbm, w_up), (down_hbm, w_down)))
    ]
    for copy in weights:
        copy.start()

    barrier = pltpu.get_barrier_semaphore()
    for peer in (sibling, across, *along):
        pl.semaphore_signal(barrier, inc=1, device_id=peer, device_id_type=pl.DeviceIdType.MESH)

    def send(src, dst, send_sem, recv_sem, peer):
        copy = pltpu.make_async_remote_copy(
            src_ref=src, dst_ref=dst, send_sem=send_sem, recv_sem=recv_sem,
            device_id=peer, device_id_type=pl.DeviceIdType.MESH,
        )
        copy.start()
        return copy

    def arrived(dst, send_sem, recv_sem):
        pltpu.make_async_remote_copy(
            src_ref=dst, dst_ref=dst, send_sem=send_sem, recv_sem=recv_sem,
            device_id=sibling, device_id_type=pl.DeviceIdType.MESH,
        ).wait_recv()

    square = (FUSED_DEVICES, FUSED_DEVICES)
    sub = lax.broadcasted_iota(jnp.int32, square, 0)
    lane = lax.broadcasted_iota(jnp.int32, square, 1)
    depth_col = jnp.sum(jnp.where(sub == lane, depths[...], 0), axis=1, keepdims=True)
    side_lane = lax.broadcasted_iota(jnp.int32, (row_count, LANES), 1)

    def route_mask(t):
        chosen = routes[t]
        hit = side_lane == chosen[:, 0:1]
        for k in range(1, top_count):
            hit = hit | (side_lane == chosen[:, k : k + 1])
        return hit

    state[...] = tokens[...].astype(jnp.float32)
    counts[...] = jnp.zeros_like(counts)

    @pl.loop(0, iter_count)
    def one_pass(t):
        state32 = state[...]
        scale = lax.rsqrt(jnp.mean(state32 * state32, axis=1, keepdims=True) + 1e-06)
        normed = (state32 * scale * gain[...].astype(jnp.float32)).astype(jnp.bfloat16)
        active = depth_col > t
        side = jnp.where(route_mask(t), 1.0, 0.0) + counts[...]
        side = jnp.where((side_lane == FLAG) & active, 1.0, side)
        mine = slot(core, y, z)
        rows = rows_all.at[t]
        rows[mine, :, :width] = normed
        rows[mine, :, width:] = side.astype(jnp.bfloat16)

        @pl.when(t == 0)
        def _():
            pl.semaphore_wait(barrier, 5)

        sent = []

        def share(at, peer):
            k = len(sent)
            sent.append(
                send(rows.at[at], rows.at[at], gather_send.at[t, k], gather_recv.at[t, at], peer)
            )

        def landed(at):
            arrived(rows.at[at], gather_send.at[t, 0], gather_recv.at[t, at])

        share(mine, across)
        for peer in (along[1], along[2], along[0]):
            share(mine, peer)
        share(mine, sibling)

        @pl.when(t == 0)
        def _():
            copy_of = choice[...]
            plan_col = jnp.sum(jnp.where(sub == lane, plan[...], 0), axis=1, keepdims=True)
            plan_at = jnp.sum(jnp.where(copy_of == sub, plan_col, 0), axis=0, keepdims=True)
            expert_row = lane[0:1]
            valid = (plan_at == expert_row) & (copy_of != expert_row)
            target = jnp.where(valid, copy_of, expert_row)
            second = valid.astype(jnp.int32)
            table = jnp.zeros((row_count, LANES), jnp.float32)
            for step in range(iter_count):
                live = jnp.where(route_mask(step) & (depth_col > step), 1.0, 0.0)
                named = jnp.sum(live, axis=0, keepdims=True)[:, :FUSED_DEVICES]
                for bit in range(2):
                    serves = (target == sub) & (second == bit)
                    column = jnp.sum(jnp.where(serves, named, 0.0), axis=1, keepdims=True)
                    table = jnp.where(side_lane == LOADS + 2 * step + bit, column, table)
            counts[...] = table

        for at_z in other_z:
            at = slot(core, y, at_z)
            landed(at)
            share(at, across)
            share(at, sibling)
        for at_z in (z, *other_z):
            at = slot(core, other_y, at_z)
            landed(at)
            share(at, sibling)
        for at_y, at_z in [(y, z)] + [(y, a) for a in other_z] + [(other_y, a) for a in (z, *other_z)]:
            landed(slot(other_core, at_y, at_z))

        @pl.when(t == 0)
        def _():
            weights[0].wait()
            weights[1].wait()

        def flat_rows():
            return rows[:, :, :width].reshape(all_rows, width)

        @pl.loop(0, hidden_width // TILE)
        def _(i):
            at = pl.ds(pl.multiple_of(i * TILE, TILE), TILE)
            x = flat_rows()
            gate_val = jnp.dot(x, w_gate[:, at], preferred_element_type=jnp.float32)
            up_val = jnp.dot(x, w_up[:, at], preferred_element_type=jnp.float32)
            silu = gate_val / (1.0 + jnp.exp(-gate_val))
            hidden[:, at] = (silu * up_val).astype(jnp.bfloat16)

        side_all = rows[:, :, width:].reshape(all_rows, LANES).astype(jnp.float32)
        logits = jnp.dot(flat_rows(), router[...], preferred_element_type=jnp.float32)
        sigma = side_all[:, :FUSED_DEVICES] / (1.0 + jnp.exp(-logits))
        gates = sigma / jnp.sum(sigma, axis=1, keepdims=True)
        all_lane = lax.broadcasted_iota(jnp.int32, (all_rows, FUSED_DEVICES), 1)
        gate_col[...] = side_all[:, FLAG : FLAG + 1] * jnp.sum(
            jnp.where(all_lane == me, gates, 0.0), axis=1, keepdims=True
        )

        @pl.when(t == iter_count - 1)
        def _():
            total = jnp.sum(rows[:, :, width:].astype(jnp.float32), axis=0)
            row_at = lax.broadcasted_iota(jnp.int32, total.shape, 0)
            own = jnp.sum(jnp.where(row_at == me, total, 0.0), axis=0, keepdims=True)
            load[...] = own[:, LOADS : LOADS + 2 * iter_count] / float(row_count * top_count)

        @pl.when(t == 0)
        def _():
            weights[2].wait()

        def to_core(c):
            span = pl.ds(other_core * half, half)
            return send(
                part.at[t, c, span], from_core.at[t, c], core_send.at[t, c], core_recv.at[t, c], sibling
            )

        def to_y(c):
            arrived(from_core.at[t, c], core_send.at[t, c], core_recv.at[t, c])
            for_y[t, c] = (
                part[t, c, pl.ds(slot(core, other_y, 0), CHIPS_Z)].astype(jnp.float32)
                + from_core[t, c, pl.ds(other_y * CHIPS_Z, CHIPS_Z)].astype(jnp.float32)
            ).astype(jnp.bfloat16)
            return send(for_y.at[t, c], from_y.at[t, c], y_send.at[t, c], y_recv.at[t, c], across)

        def summed(c, at_z):
            return (
                part[t, c, slot(core, y, at_z)].astype(jnp.float32)
                + from_core[t, c, y * CHIPS_Z + at_z].astype(jnp.float32)
                + from_y[t, c, at_z].astype(jnp.float32)
            )

        def to_z(c):
            arrived(from_y.at[t, c], y_send.at[t, c], y_recv.at[t, c])
            copies = []
            for i in (1, 2, 0):
                for_z[t, c, i] = summed(c, other_z[i]).astype(jnp.bfloat16)
                copies.append(
                    send(
                        for_z.at[t, c, i], from_z.at[t, c, i],
                        z_send.at[t, c, i], z_recv.at[t, c, i], along[i],
                    )
                )
            return copies

        def finish(c):
            total = summed(c, z)
            for i in range(CHIPS_Z - 1):
                arrived(from_z.at[t, c, i], z_send.at[t, c, i], z_recv.at[t, c, i])
                total = total + from_z[t, c, i].astype(jnp.float32)
            at = slice(c * chunk, (c + 1) * chunk)
            state[:, at] = (state[:, at] + total).astype(jnp.bfloat16).astype(jnp.float32)

        for c in range(CHUNKS):
            outs = jnp.dot(
                hidden[...], w_down[:, c * chunk : (c + 1) * chunk],
                preferred_element_type=jnp.float32,
            )
            outs = outs.astype(jnp.bfloat16).astype(jnp.float32) * gate_col[...]
            part[t, c] = outs.astype(jnp.bfloat16).reshape(FUSED_DEVICES, row_count, chunk)
            sent.append(to_core(c))
            if c >= 1:
                sent.append(to_y(c - 1))
        sent.append(to_y(CHUNKS - 1))
        for c in range(CHUNKS):
            sent.extend(to_z(c))
        for c in range(CHUNKS):
            finish(c)
        for copy in sent:
            copy.wait_send()

    out[...] = state[...].astype(jnp.bfloat16)


def fused_body(
    tokens, depths, routes, norm_gain, router, w_gate, w_up, w_down, replica_plan, copy_choice
):
    row_count, width = tokens.shape
    iter_count = routes.shape[0]
    hidden_width = w_gate.shape[2]
    all_rows = FUSED_DEVICES * row_count
    chunk = width // CHUNKS
    bf16, f32 = jnp.bfloat16, jnp.float32
    dma = pltpu.SemaphoreType.DMA
    vmem = pl.BlockSpec(memory_space=pltpu.VMEM)
    hbm = pl.BlockSpec(memory_space=pl.ANY)
    per_chunk = (iter_count, CHUNKS)
    return pl.pallas_call(
        fused_kernel,
        out_shape=(
            jax.ShapeDtypeStruct(tokens.shape, bf16),
            jax.ShapeDtypeStruct((1, 2 * iter_count), f32),
        ),
        in_specs=[vmem] * 5 + [hbm] * 3 + [vmem] * 2,
        out_specs=(vmem, vmem),
        scratch_shapes=[
            pltpu.VMEM((width, hidden_width), bf16),
            pltpu.VMEM((width, hidden_width), bf16),
            pltpu.VMEM((hidden_width, width), bf16),
            pltpu.VMEM((row_count, width), f32),
            pltpu.VMEM((row_count, LANES), f32),
            pltpu.VMEM((iter_count, FUSED_DEVICES, row_count, width + LANES), bf16),
            pltpu.VMEM((all_rows, hidden_width), bf16),
            pltpu.VMEM((all_rows, 1), f32),
            pltpu.VMEM((*per_chunk, FUSED_DEVICES, row_count, chunk), bf16),
            pltpu.VMEM((*per_chunk, CHIPS_Y * CHIPS_Z, row_count, chunk), bf16),
            pltpu.VMEM((*per_chunk, CHIPS_Z, row_count, chunk), bf16),
            pltpu.VMEM((*per_chunk, CHIPS_Z, row_count, chunk), bf16),
            pltpu.VMEM((*per_chunk, CHIPS_Z - 1, row_count, chunk), bf16),
            pltpu.VMEM((*per_chunk, CHIPS_Z - 1, row_count, chunk), bf16),
            dma((3,)),
            dma((iter_count, FUSED_DEVICES)),
            dma((iter_count, FUSED_DEVICES)),
            dma(per_chunk),
            dma(per_chunk),
            dma(per_chunk),
            dma(per_chunk),
            dma((*per_chunk, CHIPS_Z - 1)),
            dma((*per_chunk, CHIPS_Z - 1)),
        ],
        compiler_params=pltpu.CompilerParams(
            collective_id=0, has_side_effects=True, vmem_limit_bytes=48 * 1024 * 1024
        ),
        cost_estimate=pl.CostEstimate(
            flops=6 * iter_count * all_rows * width * hidden_width,
            bytes_accessed=6 * width * hidden_width,
            transcendentals=iter_count * all_rows * hidden_width,
        ),
    )(
        tokens, depths.reshape(1, -1), routes, norm_gain.reshape(1, -1), router,
        w_gate, w_up, w_down, replica_plan.reshape(1, -1), copy_choice,
    )


def expert_ffn(rows_in, gate_w, up_w, down_w):
    gate_val = jnp.dot(rows_in, gate_w, preferred_element_type=jnp.float32)
    up_val = jnp.dot(rows_in, up_w, preferred_element_type=jnp.float32)
    hidden = (jax.nn.silu(gate_val) * up_val).astype(jnp.bfloat16)
    return jnp.dot(hidden, down_w, preferred_element_type=jnp.float32).astype(jnp.bfloat16)


def dispatch_body(
    tokens, depths, routes, norm_gain, router, w_gate, w_up, w_down, replica_plan, copy_choice
):
    highest = lax.Precision.HIGHEST
    peer_count = lax.axis_size("expert")
    row_count, model_width = tokens.shape
    iter_count, _, top_count = routes.shape
    cap_rows = 2 * row_count * top_count // peer_count
    expert_ids = jnp.arange(peer_count, dtype=jnp.int32)
    copy_row = copy_choice[0]
    home_gate, home_up, home_down = (w_gate[0], w_up[0], w_down[0])
    onehot_all = routes[:, :, :, None] == expert_ids
    wanted_all = jnp.sum(jnp.where(onehot_all, copy_row, 0), axis=3)
    plan_at = jnp.sum(jnp.where(wanted_all[..., None] == expert_ids, replica_plan, 0), axis=3)
    valid_all = (plan_at == routes) & (wanted_all != routes)
    target_all = jnp.where(valid_all, wanted_all, routes)
    slot_all = valid_all.astype(jnp.int32)
    active_all = depths[None, :] > jnp.arange(iter_count, dtype=jnp.int32)[:, None]
    live_all = jnp.broadcast_to(active_all[:, :, None], routes.shape)
    bucket_all = target_all * 2 + slot_all
    bucket_hot = (bucket_all[..., None] == jnp.arange(2 * peer_count, dtype=jnp.int32)) & live_all[
        ..., None
    ]
    counts = jnp.sum(bucket_hot.astype(jnp.float32), axis=(1, 2)).reshape(iter_count, peer_count, 2)
    counts = jnp.transpose(counts, (1, 0, 2)).reshape(peer_count, 2 * iter_count)
    copy_load = lax.psum_scatter(counts, "expert", scatter_dimension=0, tiled=True) / float(
        row_count * top_count
    )
    slot_count = 1
    pair_rows = jnp.repeat(jnp.arange(row_count, dtype=jnp.int32), top_count)
    buffer_rows = peer_count * cap_rows * slot_count
    state = tokens
    for layer_step in range(iter_count):
        state32 = state.astype(jnp.float32)
        scale = lax.rsqrt(jnp.mean(state32 * state32, axis=1, keepdims=True) + 1e-06)
        normed = (state32 * scale * norm_gain.astype(jnp.float32)).astype(jnp.bfloat16)
        logits = jnp.dot(normed, router, preferred_element_type=jnp.float32)
        picked = jnp.sum(jnp.where(onehot_all[layer_step], logits[:, None, :], 0.0), axis=2)
        sigmas = jax.nn.sigmoid(picked)
        gates = sigmas / jnp.sum(sigmas, axis=1, keepdims=True)
        target_dev = routes[layer_step]
        live_pairs = live_all[layer_step].reshape(-1)
        bucket = (target_dev * slot_count).reshape(-1)
        bucket_flags = (
            (bucket[:, None] == jnp.arange(peer_count * slot_count, dtype=jnp.int32))
            & live_pairs[:, None]
        ).astype(jnp.int32)
        rank_table = jnp.cumsum(bucket_flags, axis=0)
        position = jnp.sum(rank_table * bucket_flags, axis=1) - 1
        index_flat = (target_dev.reshape(-1) * cap_rows + position) * slot_count
        send_index = jnp.where(live_pairs, index_flat, buffer_rows)
        outbound = (
            jnp.zeros((buffer_rows, model_width), jnp.bfloat16)
            .at[send_index]
            .set(normed[pair_rows], mode="drop")
        )
        outbound = outbound.reshape(peer_count, cap_rows, slot_count, model_width)
        received = lax.all_to_all(outbound, "expert", split_axis=0, concat_axis=0, tiled=True)
        count = received.shape[1]
        first_rows = received[:, :, 0, :].reshape(peer_count * count, model_width)
        result = expert_ffn(first_rows, home_gate, home_up, home_down).reshape(
            peer_count, count, 1, model_width
        )
        returned = lax.all_to_all(result, "expert", split_axis=0, concat_axis=0, tiled=True)
        read_index = jnp.where(live_pairs, index_flat, 0)
        pair_out = returned.reshape(buffer_rows, model_width)[read_index].reshape(
            row_count, top_count, model_width
        )
        weights = gates * live_all[layer_step].astype(jnp.float32)
        delta = jnp.einsum("rk,rkd->rd", weights, pair_out.astype(jnp.float32), precision=highest)
        state = (state32 + delta).astype(jnp.bfloat16)
    return (state, copy_load)


def solution(mesh):
    body = fused_body if mesh.shape["expert"] == FUSED_DEVICES else dispatch_body
    return jax.shard_map(
        body,
        mesh=mesh,
        in_specs=(
            P(("groups", "expert"), None),
            P(("groups", "expert")),
            P(None, ("groups", "expert"), None),
            P(),
            P(),
            P("expert", None, None),
            P("expert", None, None),
            P("expert", None, None),
            P(),
            P("expert", None),
        ),
        out_specs=(P(("groups", "expert"), None), P(("groups", "expert"), None)),
        check_vma=False,
    )
```

```python
import functools

import jax
import jax.numpy as jnp
from jax import lax
from jax.experimental import pallas as pl
from jax.experimental.pallas import tpu as pltpu
from jax.sharding import PartitionSpec as P

LANES = 128
FLAG = 32
LOADS = 48
CORES, CHIPS_Y, CHIPS_Z = 2, 2, 4
FUSED_DEVICES = CORES * CHIPS_Y * CHIPS_Z
CHUNKS = 4
TILE = 256


def fused_kernel(
    tokens_hbm, depths_hbm, routes_hbm, gain_hbm, plan_hbm, choice_hbm, router_hbm,
    gate_hbm, up_hbm, down_hbm,
    out, load,
    tokens, depths, routes, gain, plan, choice, router, w_gate, w_up, w_down,
    state, sides, rows_all, hidden, gate_col,
    part, from_core, for_y, from_y, for_z, from_z,
    small_sem, weight_sem, gather_send, gather_recv, core_send, core_recv, y_send, y_recv, z_send, z_recv,
):
    me = lax.axis_index("expert")
    core = me % CORES
    y = (me // CORES) % CHIPS_Y
    z = me // (CORES * CHIPS_Y)
    other_core, other_y = 1 - core, 1 - y
    other_z = (z + 1 - 2 * (z % 2), (z + 2) % CHIPS_Z, CHIPS_Z - 1 - z)

    def device(at_z, at_y, at_core):
        return {"expert": (at_z * CHIPS_Y + at_y) * CORES + at_core}

    sibling = device(z, y, other_core)
    across = device(z, other_y, core)
    along = [device(at, y, core) for at in other_z]

    iter_count, top_count, row_count = routes.shape
    width = tokens.shape[1]
    hidden_width = w_gate.shape[1]
    all_rows = FUSED_DEVICES * row_count
    chunk = width // CHUNKS
    half = CHIPS_Y * CHIPS_Z

    small = [
        pltpu.make_async_copy(src, dst, small_sem.at[i])
        for i, (src, dst) in enumerate(
            (
                (tokens_hbm, tokens), (depths_hbm, depths), (routes_hbm, routes), (gain_hbm, gain),
                (plan_hbm, plan), (choice_hbm, choice), (router_hbm, router),
            )
        )
    ]
    for copy in small:
        copy.start()
    weights = [
        pltpu.make_async_copy(src.at[0], dst, weight_sem.at[i])
        for i, (src, dst) in enumerate(((gate_hbm, w_gate), (up_hbm, w_up), (down_hbm, w_down)))
    ]
    for copy in weights:
        copy.start()

    barrier = pltpu.get_barrier_semaphore()
    for peer in (sibling, across, *along):
        pl.semaphore_signal(barrier, inc=1, device_id=peer, device_id_type=pl.DeviceIdType.MESH)

    def send(src, dst, send_sem, recv_sem, peer):
        copy = pltpu.make_async_remote_copy(
            src_ref=src, dst_ref=dst, send_sem=send_sem, recv_sem=recv_sem,
            device_id=peer, device_id_type=pl.DeviceIdType.MESH,
        )
        copy.start()
        return copy

    def arrived(dst, send_sem, recv_sem):
        pltpu.make_async_remote_copy(
            src_ref=dst, dst_ref=dst, send_sem=send_sem, recv_sem=recv_sem,
            device_id=sibling, device_id_type=pl.DeviceIdType.MESH,
        ).wait_recv()

    for copy in small:
        copy.wait()
    square = (FUSED_DEVICES, FUSED_DEVICES)
    sub = lax.broadcasted_iota(jnp.int32, square, 0)
    lane = lax.broadcasted_iota(jnp.int32, square, 1)
    side_lane = lax.broadcasted_iota(jnp.int32, (row_count, LANES), 1)
    side_sub = lax.broadcasted_iota(jnp.int32, (row_count, LANES), 0)
    diagonal = jnp.where(side_lane == side_sub, 1.0, 0.0).astype(jnp.bfloat16)
    depth_col = jnp.sum(jnp.where(sub == lane, depths[...], 0), axis=1, keepdims=True)
    state[...] = tokens[...].astype(jnp.float32)

    masks = []
    for step in range(iter_count):
        chosen = routes[step]
        hit = sub == chosen[0:1]
        for k in range(1, top_count):
            hit = hit | (sub == chosen[k : k + 1])
        masks.append(
            lax.dot_general(
                jnp.where(hit, 1.0, 0.0).astype(jnp.bfloat16), diagonal,
                (((0,), (0,)), ((), ())), preferred_element_type=jnp.float32,
            )
        )
        active = depth_col > step
        sides[step] = jnp.where((side_lane == FLAG) & active, 1.0, masks[step])

    copy_of = choice[...]
    plan_col = jnp.sum(jnp.where(sub == lane, plan[...], 0), axis=1, keepdims=True)
    plan_at = jnp.sum(jnp.where(copy_of == sub, plan_col, 0), axis=0, keepdims=True)
    expert_row = lane[0:1]
    valid = (plan_at == expert_row) & (copy_of != expert_row)
    target = jnp.where(valid, copy_of, expert_row)
    second = valid.astype(jnp.int32)
    table = sides[iter_count - 1]
    for step in range(iter_count):
        live = jnp.where(depth_col > step, masks[step], 0.0)
        named = jnp.sum(live, axis=0, keepdims=True)[:, :FUSED_DEVICES]
        for bit in range(2):
            serves = (target == sub) & (second == bit)
            column = jnp.sum(jnp.where(serves, named, 0.0), axis=1, keepdims=True)
            table = jnp.where(side_lane == LOADS + 2 * step + bit, column, table)
    sides[iter_count - 1] = table

    @pl.loop(0, iter_count)
    def one_pass(t):
        state32 = state[...]
        scale = lax.rsqrt(jnp.mean(state32 * state32, axis=1, keepdims=True) + 1e-06)
        normed = (state32 * scale * gain[...].reshape(1, width).astype(jnp.float32)).astype(jnp.bfloat16)
        rows = rows_all.at[t]
        rows[z, :, :width] = normed
        rows[z, :, width:] = sides[t].astype(jnp.bfloat16)

        @pl.when(t == 0)
        def _():
            pl.semaphore_wait(barrier, 5)

        def share(src, dst, kind, peer):
            return send(
                rows.at[src], rows.at[dst], gather_send.at[t, kind, src], gather_recv.at[t, dst], peer
            )

        def landed(at):
            arrived(rows.at[at], gather_send.at[t, 0, 0], gather_recv.at[t, at])

        def to_next(at_z, up):
            @pl.when((z < CHIPS_Z - 1) if up else (z > 0))
            def _():
                share(at_z, at_z, 0 if up else 1, device(z + 1 if up else z - 1, y, core))

        to_next(z, True)
        to_next(z, False)
        share(z, CHIPS_Z + z, 2, across)
        share(z, half + z, 3, sibling)
        for step in range(1, CHIPS_Z):
            for up in (True, False):
                at_z = z - step if up else z + step

                @pl.when((at_z >= 0) if up else (at_z < CHIPS_Z))
                def _(at_z=at_z, up=up):
                    landed(at_z)
                    to_next(at_z, up)
                    share(at_z, CHIPS_Z + at_z, 2, across)
                    share(at_z, half + at_z, 3, sibling)

        @pl.when(t == 0)
        def _():
            weights[0].wait()
            weights[1].wait()

        def half_rows(dy, lanes):
            pieces = [
                rows[pl.ds(dc * half + dy * CHIPS_Z, CHIPS_Z), :, lanes] for dc in range(CORES)
            ]
            return jnp.concatenate(pieces, axis=0).reshape(all_rows // 2, -1)

        def gate_up(dy):
            span = slice(dy * all_rows // 2, (dy + 1) * all_rows // 2)

            @pl.loop(0, hidden_width // TILE)
            def _(i):
                at = pl.ds(pl.multiple_of(i * TILE, TILE), TILE)
                x = half_rows(dy, slice(0, width))
                gate_val = jnp.dot(x, w_gate[:, at], preferred_element_type=jnp.float32)
                up_val = jnp.dot(x, w_up[:, at], preferred_element_type=jnp.float32)
                silu = gate_val / (1.0 + jnp.exp(-gate_val))
                hidden[span, at] = (silu * up_val).astype(jnp.bfloat16)

            side = half_rows(dy, slice(width, width + LANES)).astype(jnp.float32)
            logits = lax.dot_general(
                half_rows(dy, slice(0, width)), router[...],
                (((1,), (1,)), ((), ())), preferred_element_type=jnp.float32,
            )
            sigma = side[:, :FUSED_DEVICES] / (1.0 + jnp.exp(-logits))
            gates = sigma / jnp.sum(sigma, axis=1, keepdims=True)
            gate_lane = lax.broadcasted_iota(jnp.int32, gates.shape, 1)
            gate_col[span] = side[:, FLAG : FLAG + 1] * jnp.sum(
                jnp.where(gate_lane == me, gates, 0.0), axis=1, keepdims=True
            )

        for i in range(CHIPS_Z):
            landed(half + i)
        for step in range(CHIPS_Z):
            if step == 0:
                landed(CHIPS_Z + z)
                share(CHIPS_Z + z, half + CHIPS_Z + z, 3, sibling)
                continue
            for at_z, there in ((z - step, z - step >= 0), (z + step, z + step < CHIPS_Z)):

                @pl.when(there)
                def _(at_z=at_z):
                    landed(CHIPS_Z + at_z)
                    share(CHIPS_Z + at_z, half + CHIPS_Z + at_z, 3, sibling)

            if step == 1:
                gate_up(0)
        for i in range(CHIPS_Z):
            landed(half + CHIPS_Z + i)
        gate_up(1)

        @pl.when(t == iter_count - 1)
        def _():
            total = jnp.sum(rows[:, :, width:].astype(jnp.float32), axis=0)
            row_at = lax.broadcasted_iota(jnp.int32, total.shape, 0)
            own = jnp.sum(jnp.where(row_at == me, total, 0.0), axis=0, keepdims=True)
            load[...] = own[:, LOADS : LOADS + 2 * iter_count] / float(row_count * top_count)

        @pl.when(t == 0)
        def _():
            weights[2].wait()

        def to_core(c):
            return send(
                part.at[t, c, pl.ds(half, half)], from_core.at[t, c], core_send.at[t, c], core_recv.at[t, c], sibling
            )

        def to_y(c):
            arrived(from_core.at[t, c], core_send.at[t, c], core_recv.at[t, c])
            for_y[t, c] = (
                part[t, c, pl.ds(CHIPS_Z, CHIPS_Z)].astype(jnp.float32)
                + from_core[t, c, pl.ds(CHIPS_Z, CHIPS_Z)].astype(jnp.float32)
            ).astype(jnp.bfloat16)
            return send(for_y.at[t, c], from_y.at[t, c], y_send.at[t, c], y_recv.at[t, c], across)

        def summed(c, at_z):
            return (
                part[t, c, at_z].astype(jnp.float32)
                + from_core[t, c, at_z].astype(jnp.float32)
                + from_y[t, c, at_z].astype(jnp.float32)
            )

        def to_z(c):
            arrived(from_y.at[t, c], y_send.at[t, c], y_recv.at[t, c])
            copies = []
            for i in (1, 2, 0):
                for_z[t, c, i] = summed(c, other_z[i]).astype(jnp.bfloat16)
                copies.append(
                    send(
                        for_z.at[t, c, i], from_z.at[t, c, i],
                        z_send.at[t, c, i], z_recv.at[t, c, i], along[i],
                    )
                )
            return copies

        def finish(c):
            total = summed(c, z)
            for i in range(CHIPS_Z - 1):
                arrived(from_z.at[t, c, i], z_send.at[t, c, i], z_recv.at[t, c, i])
                total = total + from_z[t, c, i].astype(jnp.float32)
            at = slice(c * chunk, (c + 1) * chunk)
            state[:, at] = (state[:, at] + total).astype(jnp.bfloat16).astype(jnp.float32)

        sent = []
        for c in range(CHUNKS):
            outs = jnp.dot(
                hidden[...], w_down[:, c * chunk : (c + 1) * chunk],
                preferred_element_type=jnp.float32,
            )
            outs = outs.astype(jnp.bfloat16).astype(jnp.float32) * gate_col[...]
            outs = outs.astype(jnp.bfloat16).reshape(FUSED_DEVICES, row_count, chunk)
            for dy in range(CHIPS_Y):
                for dc in range(CORES):
                    first = (dy * CORES + dc) * CHIPS_Z
                    part[t, c, pl.ds(dc * half + dy * CHIPS_Z, CHIPS_Z)] = outs[first : first + CHIPS_Z]
            sent.append(to_core(c))
            if c >= 2:
                sent.append(to_y(c - 2))
        for c in range(CHUNKS - 2, CHUNKS):
            sent.append(to_y(c))
        for c in range(CHUNKS):
            sent.extend(to_z(c))
        for c in range(CHUNKS):
            finish(c)
        for copy in sent:
            copy.wait_send()

        def gone(src, kind):
            pltpu.make_async_remote_copy(
                src_ref=rows.at[src], dst_ref=rows.at[src],
                send_sem=gather_send.at[t, kind, src], recv_sem=gather_recv.at[t, src],
                device_id=sibling, device_id_type=pl.DeviceIdType.MESH,
            ).wait_send()

        for at_z in range(CHIPS_Z):
            pl.when((at_z <= z) & (z < CHIPS_Z - 1))(functools.partial(gone, at_z, 0))
            pl.when((at_z >= z) & (z > 0))(functools.partial(gone, at_z, 1))
            gone(at_z, 2)
            gone(at_z, 3)
            gone(CHIPS_Z + at_z, 3)

    out[...] = state[...].astype(jnp.bfloat16)


def fused_body(
    tokens, depths, routes, norm_gain, router, w_gate, w_up, w_down, replica_plan, copy_choice
):
    row_count, width = tokens.shape
    iter_count = routes.shape[0]
    hidden_width = w_gate.shape[2]
    all_rows = FUSED_DEVICES * row_count
    chunk = width // CHUNKS
    bf16, f32 = jnp.bfloat16, jnp.float32
    dma = pltpu.SemaphoreType.DMA
    vmem = pl.BlockSpec(memory_space=pltpu.VMEM)
    hbm = pl.BlockSpec(memory_space=pltpu.HBM)
    per_chunk = (iter_count, CHUNKS)
    small = (
        tokens, depths.reshape(1, -1), jnp.transpose(routes, (0, 2, 1)), norm_gain,
        replica_plan.reshape(1, -1), copy_choice, jnp.transpose(router),
    )
    return pl.pallas_call(
        fused_kernel,
        out_shape=(
            jax.ShapeDtypeStruct(tokens.shape, bf16),
            jax.ShapeDtypeStruct((1, 2 * iter_count), f32),
        ),
        in_specs=[hbm] * 10,
        out_specs=(vmem, vmem),
        scratch_shapes=[pltpu.VMEM(array.shape, array.dtype) for array in small]
        + [
            pltpu.VMEM((width, hidden_width), bf16),
            pltpu.VMEM((width, hidden_width), bf16),
            pltpu.VMEM((hidden_width, width), bf16),
            pltpu.VMEM((row_count, width), f32),
            pltpu.VMEM((iter_count, row_count, LANES), f32),
            pltpu.VMEM((iter_count, FUSED_DEVICES, row_count, width + LANES), bf16),
            pltpu.VMEM((all_rows, hidden_width), bf16),
            pltpu.VMEM((all_rows, 1), f32),
            pltpu.VMEM((*per_chunk, FUSED_DEVICES, row_count, chunk), bf16),
            pltpu.VMEM((*per_chunk, CHIPS_Y * CHIPS_Z, row_count, chunk), bf16),
            pltpu.VMEM((*per_chunk, CHIPS_Z, row_count, chunk), bf16),
            pltpu.VMEM((*per_chunk, CHIPS_Z, row_count, chunk), bf16),
            pltpu.VMEM((*per_chunk, CHIPS_Z - 1, row_count, chunk), bf16),
            pltpu.VMEM((*per_chunk, CHIPS_Z - 1, row_count, chunk), bf16),
            dma((len(small),)),
            dma((3,)),
            dma((iter_count, 4, FUSED_DEVICES)),
            dma((iter_count, FUSED_DEVICES)),
            dma(per_chunk),
            dma(per_chunk),
            dma(per_chunk),
            dma(per_chunk),
            dma((*per_chunk, CHIPS_Z - 1)),
            dma((*per_chunk, CHIPS_Z - 1)),
        ],
        compiler_params=pltpu.CompilerParams(
            collective_id=0, has_side_effects=True, vmem_limit_bytes=56 * 1024 * 1024
        ),
        cost_estimate=pl.CostEstimate(
            flops=6 * iter_count * all_rows * width * hidden_width,
            bytes_accessed=6 * width * hidden_width,
            transcendentals=iter_count * all_rows * hidden_width,
        ),
    )(
        *small, w_gate, w_up, w_down,
    )


def expert_ffn(rows_in, gate_w, up_w, down_w):
    gate_val = jnp.dot(rows_in, gate_w, preferred_element_type=jnp.float32)
    up_val = jnp.dot(rows_in, up_w, preferred_element_type=jnp.float32)
    hidden = (jax.nn.silu(gate_val) * up_val).astype(jnp.bfloat16)
    return jnp.dot(hidden, down_w, preferred_element_type=jnp.float32).astype(jnp.bfloat16)


def dispatch_body(
    tokens, depths, routes, norm_gain, router, w_gate, w_up, w_down, replica_plan, copy_choice
):
    highest = lax.Precision.HIGHEST
    peer_count = lax.axis_size("expert")
    row_count, model_width = tokens.shape
    iter_count, _, top_count = routes.shape
    cap_rows = 2 * row_count * top_count // peer_count
    expert_ids = jnp.arange(peer_count, dtype=jnp.int32)
    copy_row = copy_choice[0]
    home_gate, home_up, home_down = (w_gate[0], w_up[0], w_down[0])
    onehot_all = routes[:, :, :, None] == expert_ids
    wanted_all = jnp.sum(jnp.where(onehot_all, copy_row, 0), axis=3)
    plan_at = jnp.sum(jnp.where(wanted_all[..., None] == expert_ids, replica_plan, 0), axis=3)
    valid_all = (plan_at == routes) & (wanted_all != routes)
    target_all = jnp.where(valid_all, wanted_all, routes)
    slot_all = valid_all.astype(jnp.int32)
    active_all = depths[None, :] > jnp.arange(iter_count, dtype=jnp.int32)[:, None]
    live_all = jnp.broadcast_to(active_all[:, :, None], routes.shape)
    bucket_all = target_all * 2 + slot_all
    bucket_hot = (bucket_all[..., None] == jnp.arange(2 * peer_count, dtype=jnp.int32)) & live_all[
        ..., None
    ]
    counts = jnp.sum(bucket_hot.astype(jnp.float32), axis=(1, 2)).reshape(iter_count, peer_count, 2)
    counts = jnp.transpose(counts, (1, 0, 2)).reshape(peer_count, 2 * iter_count)
    copy_load = lax.psum_scatter(counts, "expert", scatter_dimension=0, tiled=True) / float(
        row_count * top_count
    )
    slot_count = 1
    pair_rows = jnp.repeat(jnp.arange(row_count, dtype=jnp.int32), top_count)
    buffer_rows = peer_count * cap_rows * slot_count
    state = tokens
    for layer_step in range(iter_count):
        state32 = state.astype(jnp.float32)
        scale = lax.rsqrt(jnp.mean(state32 * state32, axis=1, keepdims=True) + 1e-06)
        normed = (state32 * scale * norm_gain.astype(jnp.float32)).astype(jnp.bfloat16)
        logits = jnp.dot(normed, router, preferred_element_type=jnp.float32)
        picked = jnp.sum(jnp.where(onehot_all[layer_step], logits[:, None, :], 0.0), axis=2)
        sigmas = jax.nn.sigmoid(picked)
        gates = sigmas / jnp.sum(sigmas, axis=1, keepdims=True)
        target_dev = routes[layer_step]
        live_pairs = live_all[layer_step].reshape(-1)
        bucket = (target_dev * slot_count).reshape(-1)
        bucket_flags = (
            (bucket[:, None] == jnp.arange(peer_count * slot_count, dtype=jnp.int32))
            & live_pairs[:, None]
        ).astype(jnp.int32)
        rank_table = jnp.cumsum(bucket_flags, axis=0)
        position = jnp.sum(rank_table * bucket_flags, axis=1) - 1
        index_flat = (target_dev.reshape(-1) * cap_rows + position) * slot_count
        send_index = jnp.where(live_pairs, index_flat, buffer_rows)
        outbound = (
            jnp.zeros((buffer_rows, model_width), jnp.bfloat16)
            .at[send_index]
            .set(normed[pair_rows], mode="drop")
        )
        outbound = outbound.reshape(peer_count, cap_rows, slot_count, model_width)
        received = lax.all_to_all(outbound, "expert", split_axis=0, concat_axis=0, tiled=True)
        count = received.shape[1]
        first_rows = received[:, :, 0, :].reshape(peer_count * count, model_width)
        result = expert_ffn(first_rows, home_gate, home_up, home_down).reshape(
            peer_count, count, 1, model_width
        )
        returned = lax.all_to_all(result, "expert", split_axis=0, concat_axis=0, tiled=True)
        read_index = jnp.where(live_pairs, index_flat, 0)
        pair_out = returned.reshape(buffer_rows, model_width)[read_index].reshape(
            row_count, top_count, model_width
        )
        weights = gates * live_all[layer_step].astype(jnp.float32)
        delta = jnp.einsum("rk,rkd->rd", weights, pair_out.astype(jnp.float32), precision=highest)
        state = (state32 + delta).astype(jnp.bfloat16)
    return (state, copy_load)


def solution(mesh):
    body = fused_body if mesh.shape["expert"] == FUSED_DEVICES else dispatch_body
    return jax.shard_map(
        body,
        mesh=mesh,
        in_specs=(
            P(("groups", "expert"), None),
            P(("groups", "expert")),
            P(None, ("groups", "expert"), None),
            P(),
            P(),
            P("expert", None, None),
            P("expert", None, None),
            P("expert", None, None),
            P(),
            P("expert", None),
        ),
        out_specs=(P(("groups", "expert"), None), P(("groups", "expert"), None)),
        check_vma=False,
    )
```

```python
import functools

import jax
import jax.numpy as jnp
from jax import lax
from jax.experimental import pallas as pl
from jax.experimental.pallas import tpu as pltpu
from jax.sharding import PartitionSpec as P

LANES = 128
FLAG = 32
LOADS = 48
CORES, CHIPS_Y, CHIPS_Z = 2, 2, 4
FUSED_DEVICES = CORES * CHIPS_Y * CHIPS_Z
CHUNKS = 4
TILE = 256


def fused_kernel(
    tokens_hbm, depths_hbm, routes_hbm, gain_hbm, plan_hbm, choice_hbm, router_hbm,
    gate_hbm, up_hbm, down_hbm,
    out, load,
    tokens, depths, routes, gain, plan, choice, router, w_gate, w_up, w_down,
    state, sides, masks, rows_first, rows_second, partial, hidden, gate_col,
    part, from_core, for_y, from_y, for_z, from_z,
    small_sem, weight_sem, gather_send, gather_recv, core_send, core_recv, y_send, y_recv, z_send, z_recv,
):
    me = lax.axis_index("expert")
    core = me % CORES
    y = (me // CORES) % CHIPS_Y
    z = me // (CORES * CHIPS_Y)
    other_core, other_y = 1 - core, 1 - y
    other_z = (z + 1 - 2 * (z % 2), (z + 2) % CHIPS_Z, CHIPS_Z - 1 - z)

    def device(at_z, at_y, at_core):
        return {"expert": (at_z * CHIPS_Y + at_y) * CORES + at_core}

    sibling = device(z, y, other_core)
    across = device(z, other_y, core)
    along = [device(at, y, core) for at in other_z]

    iter_count, top_count, row_count = routes.shape
    width = tokens.shape[1]
    hidden_width = w_gate.shape[1]
    all_rows = FUSED_DEVICES * row_count
    chunk = width // CHUNKS
    half = CHIPS_Y * CHIPS_Z

    small = [
        pltpu.make_async_copy(src, dst, small_sem.at[i])
        for i, (src, dst) in enumerate(
            (
                (tokens_hbm, tokens), (depths_hbm, depths), (routes_hbm, routes), (gain_hbm, gain),
                (plan_hbm, plan), (choice_hbm, choice), (router_hbm, router),
            )
        )
    ]
    for copy in small:
        copy.start()
    weights = [
        pltpu.make_async_copy(src.at[0], dst, weight_sem.at[i])
        for i, (src, dst) in enumerate(((gate_hbm, w_gate), (up_hbm, w_up), (down_hbm, w_down)))
    ]
    for copy in weights:
        copy.start()

    barrier = pltpu.get_barrier_semaphore()
    for peer in (sibling, across, *along):
        pl.semaphore_signal(barrier, inc=1, device_id=peer, device_id_type=pl.DeviceIdType.MESH)

    def send(src, dst, send_sem, recv_sem, peer):
        copy = pltpu.make_async_remote_copy(
            src_ref=src, dst_ref=dst, send_sem=send_sem, recv_sem=recv_sem,
            device_id=peer, device_id_type=pl.DeviceIdType.MESH,
        )
        copy.start()
        return copy

    def arrived(dst, send_sem, recv_sem):
        pltpu.make_async_remote_copy(
            src_ref=dst, dst_ref=dst, send_sem=send_sem, recv_sem=recv_sem,
            device_id=sibling, device_id_type=pl.DeviceIdType.MESH,
        ).wait_recv()

    for copy in small:
        copy.wait()
    square = (FUSED_DEVICES, FUSED_DEVICES)
    sub = lax.broadcasted_iota(jnp.int32, square, 0)
    lane = lax.broadcasted_iota(jnp.int32, square, 1)
    side_lane = lax.broadcasted_iota(jnp.int32, (row_count, LANES), 1)
    side_sub = lax.broadcasted_iota(jnp.int32, (row_count, LANES), 0)
    diagonal = jnp.where(side_lane == side_sub, 1.0, 0.0).astype(jnp.bfloat16)
    depth_col = jnp.sum(jnp.where(sub == lane, depths[...], 0), axis=1, keepdims=True)
    state[...] = tokens[...].astype(jnp.float32)

    for step in range(iter_count):
        chosen = routes[step]
        hit = sub == chosen[0:1]
        for k in range(1, top_count):
            hit = hit | (sub == chosen[k : k + 1])
        masks[step] = lax.dot_general(
            jnp.where(hit, 1.0, 0.0).astype(jnp.bfloat16), diagonal,
            (((0,), (0,)), ((), ())), preferred_element_type=jnp.float32,
        )
        active = depth_col > step
        sides[step] = jnp.where((side_lane == FLAG) & active, 1.0, masks[step])

    def count_pairs():
        copy_of = choice[...]
        plan_col = jnp.sum(jnp.where(sub == lane, plan[...], 0), axis=1, keepdims=True)
        plan_at = jnp.sum(jnp.where(copy_of == sub, plan_col, 0), axis=0, keepdims=True)
        expert_row = lane[0:1]
        valid = (plan_at == expert_row) & (copy_of != expert_row)
        target = jnp.where(valid, copy_of, expert_row)
        second = valid.astype(jnp.int32)
        table = sides[iter_count - 1]
        for step in range(iter_count):
            live = jnp.where(depth_col > step, masks[step], 0.0)
            named = jnp.sum(live, axis=0, keepdims=True)[:, :FUSED_DEVICES]
            for bit in range(2):
                serves = (target == sub) & (second == bit)
                column = jnp.sum(jnp.where(serves, named, 0.0), axis=1, keepdims=True)
                table = jnp.where(side_lane == LOADS + 2 * step + bit, column, table)
        sides[iter_count - 1] = table

    @pl.loop(0, iter_count)
    def one_pass(t):
        state32 = state[...]
        scale = lax.rsqrt(jnp.mean(state32 * state32, axis=1, keepdims=True) + 1e-06)
        normed = (state32 * scale * gain[...].reshape(1, width).astype(jnp.float32)).astype(jnp.bfloat16)
        pieces = (rows_first.at[t], rows_second.at[t])
        depth = width // 2
        pieces[0][z] = normed[:, :depth]
        pieces[1][z, :, :depth] = normed[:, depth:]
        pieces[1][z, :, depth:] = sides[t].astype(jnp.bfloat16)

        @pl.when(t == 0)
        def _():
            pl.semaphore_wait(barrier, 5)

        def share(p, src, dst, kind, peer):
            return send(
                pieces[p].at[src], pieces[p].at[dst],
                gather_send.at[t, p, kind, src], gather_recv.at[t, p, dst], peer,
            )

        def landed(p, at):
            arrived(pieces[p].at[at], gather_send.at[t, p, 0, 0], gather_recv.at[t, p, at])

        def to_next(p, at_z, up):
            @pl.when((z < CHIPS_Z - 1) if up else (z > 0))
            def _():
                share(p, at_z, at_z, 0 if up else 1, device(z + 1 if up else z - 1, y, core))

        for p in range(2):
            to_next(p, z, True)
            to_next(p, z, False)
            share(p, z, CHIPS_Z + z, 2, across)
            share(p, z, half + z, 3, sibling)

        pl.when(t == 0)(count_pairs)

        for step in range(1, CHIPS_Z):
            for p in range(2):
                for up in (True, False):
                    at_z = z - step if up else z + step

                    @pl.when((at_z >= 0) if up else (at_z < CHIPS_Z))
                    def _(p=p, at_z=at_z, up=up):
                        landed(p, at_z)
                        to_next(p, at_z, up)
                        share(p, at_z, CHIPS_Z + at_z, 2, across)
                        share(p, at_z, half + at_z, 3, sibling)

        def across_to_sibling(p, step):
            ends = ((z, None),)
            if step:
                ends = ((z - step, z - step >= 0), (z + step, z + step < CHIPS_Z))
            for at_z, there in ends:

                def relay(at_z=at_z):
                    landed(p, CHIPS_Z + at_z)
                    share(p, CHIPS_Z + at_z, half + CHIPS_Z + at_z, 3, sibling)

                if there is None:
                    relay()
                else:
                    pl.when(there)(relay)

        def piece(p):
            return pieces[p][:, :, :depth].reshape(all_rows, depth)

        def gate_up(p, at):
            x = piece(p)
            span = slice(p * depth, (p + 1) * depth)
            return (
                jnp.dot(x, w_gate[span, at], preferred_element_type=jnp.float32),
                jnp.dot(x, w_up[span, at], preferred_element_type=jnp.float32),
            )

        for step in range(CHIPS_Z):
            across_to_sibling(0, step)
        for i in range(half):
            landed(0, half + i)

        @pl.when(t == 0)
        def _():
            weights[0].wait()
            weights[1].wait()

        for i in range(hidden_width // TILE):
            at = slice(i * TILE, (i + 1) * TILE)
            partial[0, :, at], partial[1, :, at] = gate_up(0, at)
            if i < CHIPS_Z:
                across_to_sibling(1, i)
        for step in range(hidden_width // TILE, CHIPS_Z):
            across_to_sibling(1, step)
        for i in range(half):
            landed(1, half + i)

        @pl.loop(0, hidden_width // TILE)
        def _(i):
            at = pl.ds(pl.multiple_of(i * TILE, TILE), TILE)
            gate_val, up_val = gate_up(1, at)
            gate_val = partial[0, :, at] + gate_val
            up_val = partial[1, :, at] + up_val
            silu = gate_val / (1.0 + jnp.exp(-gate_val))
            hidden[:, at] = (silu * up_val).astype(jnp.bfloat16)

        side = pieces[1][:, :, depth:].reshape(all_rows, LANES).astype(jnp.float32)
        logits = 0.0
        for p in range(2):
            logits += lax.dot_general(
                piece(p), router[:, p * depth : (p + 1) * depth],
                (((1,), (1,)), ((), ())), preferred_element_type=jnp.float32,
            )
        sigma = side[:, :FUSED_DEVICES] / (1.0 + jnp.exp(-logits))
        gates = sigma / jnp.sum(sigma, axis=1, keepdims=True)
        gate_lane = lax.broadcasted_iota(jnp.int32, gates.shape, 1)
        gate_col[...] = side[:, FLAG : FLAG + 1] * jnp.sum(
            jnp.where(gate_lane == me, gates, 0.0), axis=1, keepdims=True
        )

        @pl.when(t == iter_count - 1)
        def _():
            total = jnp.sum(pieces[1][:, :, depth:].astype(jnp.float32), axis=0)
            row_at = lax.broadcasted_iota(jnp.int32, total.shape, 0)
            own = jnp.sum(jnp.where(row_at == me, total, 0.0), axis=0, keepdims=True)
            load[...] = own[:, LOADS : LOADS + 2 * iter_count] / float(row_count * top_count)

        @pl.when(t == 0)
        def _():
            weights[2].wait()

        def to_core(c):
            return send(
                part.at[t, c, pl.ds(half, half)], from_core.at[t, c], core_send.at[t, c], core_recv.at[t, c], sibling
            )

        def to_y(c):
            arrived(from_core.at[t, c], core_send.at[t, c], core_recv.at[t, c])
            for_y[t, c] = (
                part[t, c, pl.ds(CHIPS_Z, CHIPS_Z)].astype(jnp.float32)
                + from_core[t, c, pl.ds(CHIPS_Z, CHIPS_Z)].astype(jnp.float32)
            ).astype(jnp.bfloat16)
            return send(for_y.at[t, c], from_y.at[t, c], y_send.at[t, c], y_recv.at[t, c], across)

        def summed(c, at_z):
            return (
                part[t, c, at_z].astype(jnp.float32)
                + from_core[t, c, at_z].astype(jnp.float32)
                + from_y[t, c, at_z].astype(jnp.float32)
            )

        def to_z(c):
            arrived(from_y.at[t, c], y_send.at[t, c], y_recv.at[t, c])
            copies = []
            for i in (1, 2, 0):
                for_z[t, c, i] = summed(c, other_z[i]).astype(jnp.bfloat16)
                copies.append(
                    send(
                        for_z.at[t, c, i], from_z.at[t, c, i],
                        z_send.at[t, c, i], z_recv.at[t, c, i], along[i],
                    )
                )
            return copies

        def finish(c):
            total = summed(c, z)
            for i in range(CHIPS_Z - 1):
                arrived(from_z.at[t, c, i], z_send.at[t, c, i], z_recv.at[t, c, i])
                total = total + from_z[t, c, i].astype(jnp.float32)
            at = slice(c * chunk, (c + 1) * chunk)
            state[:, at] = (state[:, at] + total).astype(jnp.bfloat16).astype(jnp.float32)

        sent = []
        for c in range(CHUNKS):
            outs = jnp.dot(
                hidden[...], w_down[:, c * chunk : (c + 1) * chunk],
                preferred_element_type=jnp.float32,
            )
            outs = outs.astype(jnp.bfloat16).astype(jnp.float32) * gate_col[...]
            outs = outs.astype(jnp.bfloat16).reshape(FUSED_DEVICES, row_count, chunk)
            part[t, c] = outs
            sent.append(to_core(c))
            if c >= 2:
                sent.append(to_y(c - 2))
        for c in range(CHUNKS - 2, CHUNKS):
            sent.append(to_y(c))
        for c in range(CHUNKS):
            sent.extend(to_z(c))
        for c in range(CHUNKS):
            finish(c)
        for copy in sent:
            copy.wait_send()

        def gone(p, src, kind):
            pltpu.make_async_remote_copy(
                src_ref=pieces[p].at[src], dst_ref=pieces[p].at[src],
                send_sem=gather_send.at[t, p, kind, src], recv_sem=gather_recv.at[t, p, src],
                device_id=sibling, device_id_type=pl.DeviceIdType.MESH,
            ).wait_send()

        for p in range(2):
            for at_z in range(CHIPS_Z):
                pl.when((at_z <= z) & (z < CHIPS_Z - 1))(functools.partial(gone, p, at_z, 0))
                pl.when((at_z >= z) & (z > 0))(functools.partial(gone, p, at_z, 1))
                gone(p, at_z, 2)
                gone(p, at_z, 3)
                gone(p, CHIPS_Z + at_z, 3)

    out[...] = state[...].astype(jnp.bfloat16)


def fused_body(
    tokens, depths, routes, norm_gain, router, w_gate, w_up, w_down, replica_plan, copy_choice
):
    row_count, width = tokens.shape
    iter_count = routes.shape[0]
    hidden_width = w_gate.shape[2]
    all_rows = FUSED_DEVICES * row_count
    chunk = width // CHUNKS
    bf16, f32 = jnp.bfloat16, jnp.float32
    dma = pltpu.SemaphoreType.DMA
    vmem = pl.BlockSpec(memory_space=pltpu.VMEM)
    hbm = pl.BlockSpec(memory_space=pltpu.HBM)
    per_chunk = (iter_count, CHUNKS)
    small = (
        tokens, depths.reshape(1, -1), jnp.transpose(routes, (0, 2, 1)), norm_gain,
        replica_plan.reshape(1, -1), copy_choice, jnp.transpose(router),
    )
    return pl.pallas_call(
        fused_kernel,
        out_shape=(
            jax.ShapeDtypeStruct(tokens.shape, bf16),
            jax.ShapeDtypeStruct((1, 2 * iter_count), f32),
        ),
        in_specs=[hbm] * 10,
        out_specs=(vmem, vmem),
        scratch_shapes=[pltpu.VMEM(array.shape, array.dtype) for array in small]
        + [
            pltpu.VMEM((width, hidden_width), bf16),
            pltpu.VMEM((width, hidden_width), bf16),
            pltpu.VMEM((hidden_width, width), bf16),
            pltpu.VMEM((row_count, width), f32),
            pltpu.VMEM((iter_count, row_count, LANES), f32),
            pltpu.VMEM((iter_count, row_count, LANES), f32),
            pltpu.VMEM((iter_count, FUSED_DEVICES, row_count, width // 2), bf16),
            pltpu.VMEM((iter_count, FUSED_DEVICES, row_count, width // 2 + LANES), bf16),
            pltpu.VMEM((2, all_rows, hidden_width), f32),
            pltpu.VMEM((all_rows, hidden_width), bf16),
            pltpu.VMEM((all_rows, 1), f32),
            pltpu.VMEM((*per_chunk, FUSED_DEVICES, row_count, chunk), bf16),
            pltpu.VMEM((*per_chunk, CHIPS_Y * CHIPS_Z, row_count, chunk), bf16),
            pltpu.VMEM((*per_chunk, CHIPS_Z, row_count, chunk), bf16),
            pltpu.VMEM((*per_chunk, CHIPS_Z, row_count, chunk), bf16),
            pltpu.VMEM((*per_chunk, CHIPS_Z - 1, row_count, chunk), bf16),
            pltpu.VMEM((*per_chunk, CHIPS_Z - 1, row_count, chunk), bf16),
            dma((len(small),)),
            dma((3,)),
            dma((iter_count, 2, 4, FUSED_DEVICES)),
            dma((iter_count, 2, FUSED_DEVICES)),
            dma(per_chunk),
            dma(per_chunk),
            dma(per_chunk),
            dma(per_chunk),
            dma((*per_chunk, CHIPS_Z - 1)),
            dma((*per_chunk, CHIPS_Z - 1)),
        ],
        compiler_params=pltpu.CompilerParams(
            collective_id=0, has_side_effects=True, vmem_limit_bytes=56 * 1024 * 1024
        ),
        cost_estimate=pl.CostEstimate(
            flops=6 * iter_count * all_rows * width * hidden_width,
            bytes_accessed=6 * width * hidden_width,
            transcendentals=iter_count * all_rows * hidden_width,
        ),
    )(
        *small, w_gate, w_up, w_down,
    )


def expert_ffn(rows_in, gate_w, up_w, down_w):
    gate_val = jnp.dot(rows_in, gate_w, preferred_element_type=jnp.float32)
    up_val = jnp.dot(rows_in, up_w, preferred_element_type=jnp.float32)
    hidden = (jax.nn.silu(gate_val) * up_val).astype(jnp.bfloat16)
    return jnp.dot(hidden, down_w, preferred_element_type=jnp.float32).astype(jnp.bfloat16)


def dispatch_body(
    tokens, depths, routes, norm_gain, router, w_gate, w_up, w_down, replica_plan, copy_choice
):
    highest = lax.Precision.HIGHEST
    peer_count = lax.axis_size("expert")
    row_count, model_width = tokens.shape
    iter_count, _, top_count = routes.shape
    cap_rows = 2 * row_count * top_count // peer_count
    expert_ids = jnp.arange(peer_count, dtype=jnp.int32)
    copy_row = copy_choice[0]
    home_gate, home_up, home_down = (w_gate[0], w_up[0], w_down[0])
    onehot_all = routes[:, :, :, None] == expert_ids
    wanted_all = jnp.sum(jnp.where(onehot_all, copy_row, 0), axis=3)
    plan_at = jnp.sum(jnp.where(wanted_all[..., None] == expert_ids, replica_plan, 0), axis=3)
    valid_all = (plan_at == routes) & (wanted_all != routes)
    target_all = jnp.where(valid_all, wanted_all, routes)
    slot_all = valid_all.astype(jnp.int32)
    active_all = depths[None, :] > jnp.arange(iter_count, dtype=jnp.int32)[:, None]
    live_all = jnp.broadcast_to(active_all[:, :, None], routes.shape)
    bucket_all = target_all * 2 + slot_all
    bucket_hot = (bucket_all[..., None] == jnp.arange(2 * peer_count, dtype=jnp.int32)) & live_all[
        ..., None
    ]
    counts = jnp.sum(bucket_hot.astype(jnp.float32), axis=(1, 2)).reshape(iter_count, peer_count, 2)
    counts = jnp.transpose(counts, (1, 0, 2)).reshape(peer_count, 2 * iter_count)
    copy_load = lax.psum_scatter(counts, "expert", scatter_dimension=0, tiled=True) / float(
        row_count * top_count
    )
    slot_count = 1
    pair_rows = jnp.repeat(jnp.arange(row_count, dtype=jnp.int32), top_count)
    buffer_rows = peer_count * cap_rows * slot_count
    state = tokens
    for layer_step in range(iter_count):
        state32 = state.astype(jnp.float32)
        scale = lax.rsqrt(jnp.mean(state32 * state32, axis=1, keepdims=True) + 1e-06)
        normed = (state32 * scale * norm_gain.astype(jnp.float32)).astype(jnp.bfloat16)
        logits = jnp.dot(normed, router, preferred_element_type=jnp.float32)
        picked = jnp.sum(jnp.where(onehot_all[layer_step], logits[:, None, :], 0.0), axis=2)
        sigmas = jax.nn.sigmoid(picked)
        gates = sigmas / jnp.sum(sigmas, axis=1, keepdims=True)
        target_dev = routes[layer_step]
        live_pairs = live_all[layer_step].reshape(-1)
        bucket = (target_dev * slot_count).reshape(-1)
        bucket_flags = (
            (bucket[:, None] == jnp.arange(peer_count * slot_count, dtype=jnp.int32))
            & live_pairs[:, None]
        ).astype(jnp.int32)
        rank_table = jnp.cumsum(bucket_flags, axis=0)
        position = jnp.sum(rank_table * bucket_flags, axis=1) - 1
        index_flat = (target_dev.reshape(-1) * cap_rows + position) * slot_count
        send_index = jnp.where(live_pairs, index_flat, buffer_rows)
        outbound = (
            jnp.zeros((buffer_rows, model_width), jnp.bfloat16)
            .at[send_index]
            .set(normed[pair_rows], mode="drop")
        )
        outbound = outbound.reshape(peer_count, cap_rows, slot_count, model_width)
        received = lax.all_to_all(outbound, "expert", split_axis=0, concat_axis=0, tiled=True)
        count = received.shape[1]
        first_rows = received[:, :, 0, :].reshape(peer_count * count, model_width)
        result = expert_ffn(first_rows, home_gate, home_up, home_down).reshape(
            peer_count, count, 1, model_width
        )
        returned = lax.all_to_all(result, "expert", split_axis=0, concat_axis=0, tiled=True)
        read_index = jnp.where(live_pairs, index_flat, 0)
        pair_out = returned.reshape(buffer_rows, model_width)[read_index].reshape(
            row_count, top_count, model_width
        )
        weights = gates * live_all[layer_step].astype(jnp.float32)
        delta = jnp.einsum("rk,rkd->rd", weights, pair_out.astype(jnp.float32), precision=highest)
        state = (state32 + delta).astype(jnp.bfloat16)
    return (state, copy_load)


def solution(mesh):
    body = fused_body if mesh.shape["expert"] == FUSED_DEVICES else dispatch_body
    return jax.shard_map(
        body,
        mesh=mesh,
        in_specs=(
            P(("groups", "expert"), None),
            P(("groups", "expert")),
            P(None, ("groups", "expert"), None),
            P(),
            P(),
            P("expert", None, None),
            P("expert", None, None),
            P("expert", None, None),
            P(),
            P("expert", None),
        ),
        out_specs=(P(("groups", "expert"), None), P(("groups", "expert"), None)),
        check_vma=False,
    )
```

```python
import jax
import jax.numpy as jnp
from jax import lax
from jax.experimental import pallas as pl
from jax.experimental.pallas import tpu as pltpu
from jax.sharding import PartitionSpec as P

LANES = 128
FLAG = 32
LOADS = 48
CORES, CHIPS_Y, CHIPS_Z = 2, 2, 4
FUSED_DEVICES = CORES * CHIPS_Y * CHIPS_Z
CHUNKS = 2
TILE = 256


def fused_kernel(
    tokens_hbm, depths_hbm, routes_hbm, gain_hbm, plan_hbm, choice_hbm, router_hbm,
    gate_hbm, up_hbm, down_hbm,
    out, load,
    tokens, depths, routes, gain, plan, choice, router, w_gate, w_up, w_down,
    state, sides, masks, rows_all, hidden, gate_col,
    part, from_core, for_y, from_y, for_z, from_z,
    small_sem, weight_sem, gather_send, gather_recv, core_send, core_recv, y_send, y_recv, z_send, z_recv,
):
    me = lax.axis_index("expert")
    core = me % CORES
    y = (me // CORES) % CHIPS_Y
    z = me // (CORES * CHIPS_Y)
    other_core, other_y = 1 - core, 1 - y
    other_z = (z + 1 - 2 * (z % 2), (z + 2) % CHIPS_Z, CHIPS_Z - 1 - z)

    def device(at_z, at_y, at_core):
        return {"expert": (at_z * CHIPS_Y + at_y) * CORES + at_core}

    sibling = device(z, y, other_core)
    across = device(z, other_y, core)
    along = [device(at, y, core) for at in other_z]

    iter_count, top_count, row_count = routes.shape
    width = tokens.shape[1]
    hidden_width = w_gate.shape[1]
    all_rows = FUSED_DEVICES * row_count
    chunk = width // CHUNKS
    half = CHIPS_Y * CHIPS_Z

    small = [
        pltpu.make_async_copy(src, dst, small_sem.at[i])
        for i, (src, dst) in enumerate(
            (
                (tokens_hbm, tokens), (depths_hbm, depths), (routes_hbm, routes), (gain_hbm, gain),
                (plan_hbm, plan), (choice_hbm, choice), (router_hbm, router),
            )
        )
    ]
    for copy in small:
        copy.start()
    weights = [
        pltpu.make_async_copy(src.at[0], dst, weight_sem.at[i])
        for i, (src, dst) in enumerate(((gate_hbm, w_gate), (up_hbm, w_up), (down_hbm, w_down)))
    ]
    for copy in weights:
        copy.start()

    barrier = pltpu.get_barrier_semaphore()
    for peer in (sibling, across, *along):
        pl.semaphore_signal(barrier, inc=1, device_id=peer, device_id_type=pl.DeviceIdType.MESH)

    def send(src, dst, send_sem, recv_sem, peer):
        copy = pltpu.make_async_remote_copy(
            src_ref=src, dst_ref=dst, send_sem=send_sem, recv_sem=recv_sem,
            device_id=peer, device_id_type=pl.DeviceIdType.MESH,
        )
        copy.start()
        return copy

    def arrived(dst, send_sem, recv_sem):
        pltpu.make_async_remote_copy(
            src_ref=dst, dst_ref=dst, send_sem=send_sem, recv_sem=recv_sem,
            device_id=sibling, device_id_type=pl.DeviceIdType.MESH,
        ).wait_recv()

    for copy in small:
        copy.wait()
    square = (FUSED_DEVICES, FUSED_DEVICES)
    sub = lax.broadcasted_iota(jnp.int32, square, 0)
    lane = lax.broadcasted_iota(jnp.int32, square, 1)
    side_lane = lax.broadcasted_iota(jnp.int32, (row_count, LANES), 1)
    side_sub = lax.broadcasted_iota(jnp.int32, (row_count, LANES), 0)
    diagonal = jnp.where(side_lane == side_sub, 1.0, 0.0).astype(jnp.bfloat16)
    depth_col = jnp.sum(jnp.where(sub == lane, depths[...], 0), axis=1, keepdims=True)
    state[...] = tokens[...].astype(jnp.float32)

    for step in range(iter_count):
        chosen = routes[step]
        hit = sub == chosen[0:1]
        for k in range(1, top_count):
            hit = hit | (sub == chosen[k : k + 1])
        masks[step] = lax.dot_general(
            jnp.where(hit, 1.0, 0.0).astype(jnp.bfloat16), diagonal,
            (((0,), (0,)), ((), ())), preferred_element_type=jnp.float32,
        )
        active = depth_col > step
        sides[step] = jnp.where((side_lane == FLAG) & active, 1.0, masks[step])

    def count_pairs():
        copy_of = choice[...]
        plan_col = jnp.sum(jnp.where(sub == lane, plan[...], 0), axis=1, keepdims=True)
        plan_at = jnp.sum(jnp.where(copy_of == sub, plan_col, 0), axis=0, keepdims=True)
        expert_row = lane[0:1]
        valid = (plan_at == expert_row) & (copy_of != expert_row)
        target = jnp.where(valid, copy_of, expert_row)
        second = valid.astype(jnp.int32)
        table = sides[iter_count - 1]
        for step in range(iter_count):
            live = jnp.where(depth_col > step, masks[step], 0.0)
            named = jnp.sum(live, axis=0, keepdims=True)[:, :FUSED_DEVICES]
            for bit in range(2):
                serves = (target == sub) & (second == bit)
                column = jnp.sum(jnp.where(serves, named, 0.0), axis=1, keepdims=True)
                table = jnp.where(side_lane == LOADS + 2 * step + bit, column, table)
        sides[iter_count - 1] = table

    @pl.loop(0, iter_count)
    def one_pass(t):
        state32 = state[...]
        scale = lax.rsqrt(jnp.mean(state32 * state32, axis=1, keepdims=True) + 1e-06)
        normed = (state32 * scale * gain[...].reshape(1, width).astype(jnp.float32)).astype(jnp.bfloat16)
        rows = rows_all.at[t]
        rows[z, :, :width] = normed
        rows[z, :, width:] = sides[t].astype(jnp.bfloat16)

        @pl.when(t == 0)
        def _():
            pl.semaphore_wait(barrier, 5)

        sent = []

        def share(src, dst, peer, blocks=1):
            k = len(sent)
            sent.append(
                send(
                    rows.at[pl.ds(src, blocks)], rows.at[pl.ds(dst, blocks)],
                    gather_send.at[t, k], gather_recv.at[t, dst], peer,
                )
            )

        def landed(at, blocks=1):
            arrived(rows.at[pl.ds(at, blocks)], gather_send.at[t, 0], gather_recv.at[t, at])

        share(z, CHIPS_Z + z, across)
        for peer in along:
            share(z, z, peer)
        pl.when(t == 0)(count_pairs)
        for at_z in other_z:
            landed(at_z)
            share(at_z, CHIPS_Z + at_z, across)
        share(0, half, sibling, CHIPS_Z)
        for at_z in (z, *other_z):
            landed(CHIPS_Z + at_z)
        share(CHIPS_Z, half + CHIPS_Z, sibling, CHIPS_Z)

        @pl.when(t == 0)
        def _():
            weights[0].wait()
            weights[1].wait()

        for dy in range(CHIPS_Y):
            landed(half + dy * CHIPS_Z, CHIPS_Z)

        def flat_rows():
            return rows[:, :, :width].reshape(all_rows, width)

        @pl.loop(0, hidden_width // TILE)
        def _(i):
            at = pl.ds(pl.multiple_of(i * TILE, TILE), TILE)
            x = flat_rows()
            gate_val = jnp.dot(x, w_gate[:, at], preferred_element_type=jnp.float32)
            up_val = jnp.dot(x, w_up[:, at], preferred_element_type=jnp.float32)
            silu = gate_val / (1.0 + jnp.exp(-gate_val))
            hidden[:, at] = (silu * up_val).astype(jnp.bfloat16)

        side = rows[:, :, width:].reshape(all_rows, LANES).astype(jnp.float32)
        logits = lax.dot_general(
            flat_rows(), router[...], (((1,), (1,)), ((), ())), preferred_element_type=jnp.float32
        )
        sigma = side[:, :FUSED_DEVICES] / (1.0 + jnp.exp(-logits))
        gates = sigma / jnp.sum(sigma, axis=1, keepdims=True)
        gate_lane = lax.broadcasted_iota(jnp.int32, gates.shape, 1)
        gate_col[...] = side[:, FLAG : FLAG + 1] * jnp.sum(
            jnp.where(gate_lane == me, gates, 0.0), axis=1, keepdims=True
        )

        @pl.when(t == iter_count - 1)
        def _():
            total = jnp.sum(rows[:, :, width:].astype(jnp.float32), axis=0)
            row_at = lax.broadcasted_iota(jnp.int32, total.shape, 0)
            own = jnp.sum(jnp.where(row_at == me, total, 0.0), axis=0, keepdims=True)
            load[...] = own[:, LOADS : LOADS + 2 * iter_count] / float(row_count * top_count)

        @pl.when(t == 0)
        def _():
            weights[2].wait()

        def to_core(c):
            return send(
                part.at[t, c, pl.ds(half, half)], from_core.at[t, c], core_send.at[t, c], core_recv.at[t, c], sibling
            )

        def to_y(c):
            arrived(from_core.at[t, c], core_send.at[t, c], core_recv.at[t, c])
            for_y[t, c] = (
                part[t, c, pl.ds(CHIPS_Z, CHIPS_Z)].astype(jnp.float32)
                + from_core[t, c, pl.ds(CHIPS_Z, CHIPS_Z)].astype(jnp.float32)
            ).astype(jnp.bfloat16)
            return send(for_y.at[t, c], from_y.at[t, c], y_send.at[t, c], y_recv.at[t, c], across)

        def summed(c, at_z):
            return (
                part[t, c, at_z].astype(jnp.float32)
                + from_core[t, c, at_z].astype(jnp.float32)
                + from_y[t, c, at_z].astype(jnp.float32)
            )

        def to_z(c):
            arrived(from_y.at[t, c], y_send.at[t, c], y_recv.at[t, c])
            copies = []
            for i in (1, 2, 0):
                for_z[t, c, i] = summed(c, other_z[i]).astype(jnp.bfloat16)
                copies.append(
                    send(
                        for_z.at[t, c, i], from_z.at[t, c, i],
                        z_send.at[t, c, i], z_recv.at[t, c, i], along[i],
                    )
                )
            return copies

        def finish(c):
            total = summed(c, z)
            for i in range(CHIPS_Z - 1):
                arrived(from_z.at[t, c, i], z_send.at[t, c, i], z_recv.at[t, c, i])
                total = total + from_z[t, c, i].astype(jnp.float32)
            at = slice(c * chunk, (c + 1) * chunk)
            state[:, at] = (state[:, at] + total).astype(jnp.bfloat16).astype(jnp.float32)

        for c in range(CHUNKS):
            outs = jnp.dot(
                hidden[...], w_down[:, c * chunk : (c + 1) * chunk],
                preferred_element_type=jnp.float32,
            )
            outs = outs.astype(jnp.bfloat16).astype(jnp.float32) * gate_col[...]
            outs = outs.astype(jnp.bfloat16).reshape(FUSED_DEVICES, row_count, chunk)
            part[t, c] = outs
            sent.append(to_core(c))
            if c >= 1:
                sent.append(to_y(c - 1))
        sent.append(to_y(CHUNKS - 1))
        for c in range(CHUNKS):
            sent.extend(to_z(c))
        for c in range(CHUNKS):
            finish(c)
        for copy in sent:
            copy.wait_send()

    out[...] = state[...].astype(jnp.bfloat16)


def fused_body(
    tokens, depths, routes, norm_gain, router, w_gate, w_up, w_down, replica_plan, copy_choice
):
    row_count, width = tokens.shape
    iter_count = routes.shape[0]
    hidden_width = w_gate.shape[2]
    all_rows = FUSED_DEVICES * row_count
    chunk = width // CHUNKS
    bf16, f32 = jnp.bfloat16, jnp.float32
    dma = pltpu.SemaphoreType.DMA
    vmem = pl.BlockSpec(memory_space=pltpu.VMEM)
    hbm = pl.BlockSpec(memory_space=pltpu.HBM)
    per_chunk = (iter_count, CHUNKS)
    small = (
        tokens, depths.reshape(1, -1), jnp.transpose(routes, (0, 2, 1)), norm_gain,
        replica_plan.reshape(1, -1), copy_choice, jnp.transpose(router),
    )
    return pl.pallas_call(
        fused_kernel,
        out_shape=(
            jax.ShapeDtypeStruct(tokens.shape, bf16),
            jax.ShapeDtypeStruct((1, 2 * iter_count), f32),
        ),
        in_specs=[hbm] * 10,
        out_specs=(vmem, vmem),
        scratch_shapes=[pltpu.VMEM(array.shape, array.dtype) for array in small]
        + [
            pltpu.VMEM((width, hidden_width), bf16),
            pltpu.VMEM((width, hidden_width), bf16),
            pltpu.VMEM((hidden_width, width), bf16),
            pltpu.VMEM((row_count, width), f32),
            pltpu.VMEM((iter_count, row_count, LANES), f32),
            pltpu.VMEM((iter_count, row_count, LANES), f32),
            pltpu.VMEM((iter_count, FUSED_DEVICES, row_count, width + LANES), bf16),
            pltpu.VMEM((all_rows, hidden_width), bf16),
            pltpu.VMEM((all_rows, 1), f32),
            pltpu.VMEM((*per_chunk, FUSED_DEVICES, row_count, chunk), bf16),
            pltpu.VMEM((*per_chunk, CHIPS_Y * CHIPS_Z, row_count, chunk), bf16),
            pltpu.VMEM((*per_chunk, CHIPS_Z, row_count, chunk), bf16),
            pltpu.VMEM((*per_chunk, CHIPS_Z, row_count, chunk), bf16),
            pltpu.VMEM((*per_chunk, CHIPS_Z - 1, row_count, chunk), bf16),
            pltpu.VMEM((*per_chunk, CHIPS_Z - 1, row_count, chunk), bf16),
            dma((len(small),)),
            dma((3,)),
            dma((iter_count, FUSED_DEVICES)),
            dma((iter_count, FUSED_DEVICES)),
            dma(per_chunk),
            dma(per_chunk),
            dma(per_chunk),
            dma(per_chunk),
            dma((*per_chunk, CHIPS_Z - 1)),
            dma((*per_chunk, CHIPS_Z - 1)),
        ],
        compiler_params=pltpu.CompilerParams(
            collective_id=0, has_side_effects=True, vmem_limit_bytes=56 * 1024 * 1024
        ),
        cost_estimate=pl.CostEstimate(
            flops=6 * iter_count * all_rows * width * hidden_width,
            bytes_accessed=6 * width * hidden_width,
            transcendentals=iter_count * all_rows * hidden_width,
        ),
    )(
        *small, w_gate, w_up, w_down,
    )


def expert_ffn(rows_in, gate_w, up_w, down_w):
    gate_val = jnp.dot(rows_in, gate_w, preferred_element_type=jnp.float32)
    up_val = jnp.dot(rows_in, up_w, preferred_element_type=jnp.float32)
    hidden = (jax.nn.silu(gate_val) * up_val).astype(jnp.bfloat16)
    return jnp.dot(hidden, down_w, preferred_element_type=jnp.float32).astype(jnp.bfloat16)


def dispatch_body(
    tokens, depths, routes, norm_gain, router, w_gate, w_up, w_down, replica_plan, copy_choice
):
    highest = lax.Precision.HIGHEST
    peer_count = lax.axis_size("expert")
    row_count, model_width = tokens.shape
    iter_count, _, top_count = routes.shape
    cap_rows = 2 * row_count * top_count // peer_count
    expert_ids = jnp.arange(peer_count, dtype=jnp.int32)
    copy_row = copy_choice[0]
    home_gate, home_up, home_down = (w_gate[0], w_up[0], w_down[0])
    onehot_all = routes[:, :, :, None] == expert_ids
    wanted_all = jnp.sum(jnp.where(onehot_all, copy_row, 0), axis=3)
    plan_at = jnp.sum(jnp.where(wanted_all[..., None] == expert_ids, replica_plan, 0), axis=3)
    valid_all = (plan_at == routes) & (wanted_all != routes)
    target_all = jnp.where(valid_all, wanted_all, routes)
    slot_all = valid_all.astype(jnp.int32)
    active_all = depths[None, :] > jnp.arange(iter_count, dtype=jnp.int32)[:, None]
    live_all = jnp.broadcast_to(active_all[:, :, None], routes.shape)
    bucket_all = target_all * 2 + slot_all
    bucket_hot = (bucket_all[..., None] == jnp.arange(2 * peer_count, dtype=jnp.int32)) & live_all[
        ..., None
    ]
    counts = jnp.sum(bucket_hot.astype(jnp.float32), axis=(1, 2)).reshape(iter_count, peer_count, 2)
    counts = jnp.transpose(counts, (1, 0, 2)).reshape(peer_count, 2 * iter_count)
    copy_load = lax.psum_scatter(counts, "expert", scatter_dimension=0, tiled=True) / float(
        row_count * top_count
    )
    slot_count = 1
    pair_rows = jnp.repeat(jnp.arange(row_count, dtype=jnp.int32), top_count)
    buffer_rows = peer_count * cap_rows * slot_count
    state = tokens
    for layer_step in range(iter_count):
        state32 = state.astype(jnp.float32)
        scale = lax.rsqrt(jnp.mean(state32 * state32, axis=1, keepdims=True) + 1e-06)
        normed = (state32 * scale * norm_gain.astype(jnp.float32)).astype(jnp.bfloat16)
        logits = jnp.dot(normed, router, preferred_element_type=jnp.float32)
        picked = jnp.sum(jnp.where(onehot_all[layer_step], logits[:, None, :], 0.0), axis=2)
        sigmas = jax.nn.sigmoid(picked)
        gates = sigmas / jnp.sum(sigmas, axis=1, keepdims=True)
        target_dev = routes[layer_step]
        live_pairs = live_all[layer_step].reshape(-1)
        bucket = (target_dev * slot_count).reshape(-1)
        bucket_flags = (
            (bucket[:, None] == jnp.arange(peer_count * slot_count, dtype=jnp.int32))
            & live_pairs[:, None]
        ).astype(jnp.int32)
        rank_table = jnp.cumsum(bucket_flags, axis=0)
        position = jnp.sum(rank_table * bucket_flags, axis=1) - 1
        index_flat = (target_dev.reshape(-1) * cap_rows + position) * slot_count
        send_index = jnp.where(live_pairs, index_flat, buffer_rows)
        outbound = (
            jnp.zeros((buffer_rows, model_width), jnp.bfloat16)
            .at[send_index]
            .set(normed[pair_rows], mode="drop")
        )
        outbound = outbound.reshape(peer_count, cap_rows, slot_count, model_width)
        received = lax.all_to_all(outbound, "expert", split_axis=0, concat_axis=0, tiled=True)
        count = received.shape[1]
        first_rows = received[:, :, 0, :].reshape(peer_count * count, model_width)
        result = expert_ffn(first_rows, home_gate, home_up, home_down).reshape(
            peer_count, count, 1, model_width
        )
        returned = lax.all_to_all(result, "expert", split_axis=0, concat_axis=0, tiled=True)
        read_index = jnp.where(live_pairs, index_flat, 0)
        pair_out = returned.reshape(buffer_rows, model_width)[read_index].reshape(
            row_count, top_count, model_width
        )
        weights = gates * live_all[layer_step].astype(jnp.float32)
        delta = jnp.einsum("rk,rkd->rd", weights, pair_out.astype(jnp.float32), precision=highest)
        state = (state32 + delta).astype(jnp.bfloat16)
    return (state, copy_load)


def solution(mesh):
    body = fused_body if mesh.shape["expert"] == FUSED_DEVICES else dispatch_body
    return jax.shard_map(
        body,
        mesh=mesh,
        in_specs=(
            P(("groups", "expert"), None),
            P(("groups", "expert")),
            P(None, ("groups", "expert"), None),
            P(),
            P(),
            P("expert", None, None),
            P("expert", None, None),
            P("expert", None, None),
            P(),
            P("expert", None),
        ),
        out_specs=(P(("groups", "expert"), None), P(("groups", "expert"), None)),
        check_vma=False,
    )
```

```python
import jax
import jax.numpy as jnp
from jax import lax
from jax.experimental import pallas as pl
from jax.experimental.pallas import tpu as pltpu
from jax.sharding import PartitionSpec as P

LANES = 128
FLAG = 32
LOADS = 48
CORES, CHIPS_Y, CHIPS_Z = 2, 2, 4
FUSED_DEVICES = CORES * CHIPS_Y * CHIPS_Z
CHUNKS = 4
TILE = 256


def fused_kernel(
    tokens_hbm, depths_hbm, routes_hbm, gain_hbm, plan_hbm, choice_hbm, router_hbm,
    gate_hbm, up_hbm, down_hbm,
    out, load,
    tokens, depths, routes, gain, plan, choice, router, w_gate, w_up, w_down,
    state, sides, masks, rows_all, hidden, gate_col,
    part, from_core, for_y, from_y, for_z, from_z,
    small_sem, weight_sem, gather_send, gather_recv, core_send, core_recv, y_send, y_recv, z_send, z_recv,
):
    me = lax.axis_index("expert")
    core = me % CORES
    y = (me // CORES) % CHIPS_Y
    z = me // (CORES * CHIPS_Y)
    other_core, other_y = 1 - core, 1 - y
    other_z = (z + 1 - 2 * (z % 2), (z + 2) % CHIPS_Z, CHIPS_Z - 1 - z)

    def device(at_z, at_y, at_core):
        return {"expert": (at_z * CHIPS_Y + at_y) * CORES + at_core}

    sibling = device(z, y, other_core)
    across = device(z, other_y, core)
    along = [device(at, y, core) for at in other_z]

    iter_count, top_count, row_count = routes.shape
    width = tokens.shape[1]
    hidden_width = w_gate.shape[1]
    all_rows = FUSED_DEVICES * row_count
    chunk = width // CHUNKS
    half = CHIPS_Y * CHIPS_Z

    small = [
        pltpu.make_async_copy(src, dst, small_sem.at[i])
        for i, (src, dst) in enumerate(
            (
                (tokens_hbm, tokens), (depths_hbm, depths), (routes_hbm, routes), (gain_hbm, gain),
                (plan_hbm, plan), (choice_hbm, choice), (router_hbm, router),
            )
        )
    ]
    for copy in small:
        copy.start()
    weights = [
        pltpu.make_async_copy(src.at[0], dst, weight_sem.at[i])
        for i, (src, dst) in enumerate(((gate_hbm, w_gate), (up_hbm, w_up), (down_hbm, w_down)))
    ]
    for copy in weights:
        copy.start()

    barrier = pltpu.get_barrier_semaphore()
    for peer in (sibling, across, *along):
        pl.semaphore_signal(barrier, inc=1, device_id=peer, device_id_type=pl.DeviceIdType.MESH)

    def send(src, dst, send_sem, recv_sem, peer):
        copy = pltpu.make_async_remote_copy(
            src_ref=src, dst_ref=dst, send_sem=send_sem, recv_sem=recv_sem,
            device_id=peer, device_id_type=pl.DeviceIdType.MESH,
        )
        copy.start()
        return copy

    def arrived(dst, send_sem, recv_sem):
        pltpu.make_async_remote_copy(
            src_ref=dst, dst_ref=dst, send_sem=send_sem, recv_sem=recv_sem,
            device_id=sibling, device_id_type=pl.DeviceIdType.MESH,
        ).wait_recv()

    for copy in small:
        copy.wait()
    square = (FUSED_DEVICES, FUSED_DEVICES)
    sub = lax.broadcasted_iota(jnp.int32, square, 0)
    lane = lax.broadcasted_iota(jnp.int32, square, 1)
    side_lane = lax.broadcasted_iota(jnp.int32, (row_count, LANES), 1)
    side_sub = lax.broadcasted_iota(jnp.int32, (row_count, LANES), 0)
    diagonal = jnp.where(side_lane == side_sub, 1.0, 0.0).astype(jnp.bfloat16)
    depth_col = jnp.sum(jnp.where(sub == lane, depths[...], 0), axis=1, keepdims=True)
    state[...] = tokens[...].astype(jnp.float32)

    for step in range(iter_count):
        chosen = routes[step]
        hit = sub == chosen[0:1]
        for k in range(1, top_count):
            hit = hit | (sub == chosen[k : k + 1])
        masks[step] = lax.dot_general(
            jnp.where(hit, 1.0, 0.0).astype(jnp.bfloat16), diagonal,
            (((0,), (0,)), ((), ())), preferred_element_type=jnp.float32,
        )
        active = depth_col > step
        sides[step] = jnp.where((side_lane == FLAG) & active, 1.0, masks[step])

    def count_pairs():
        copy_of = choice[...]
        plan_col = jnp.sum(jnp.where(sub == lane, plan[...], 0), axis=1, keepdims=True)
        plan_at = jnp.sum(jnp.where(copy_of == sub, plan_col, 0), axis=0, keepdims=True)
        expert_row = lane[0:1]
        valid = (plan_at == expert_row) & (copy_of != expert_row)
        target = jnp.where(valid, copy_of, expert_row)
        second = valid.astype(jnp.int32)
        table = sides[iter_count - 1]
        for step in range(iter_count):
            live = jnp.where(depth_col > step, masks[step], 0.0)
            named = jnp.sum(live, axis=0, keepdims=True)[:, :FUSED_DEVICES]
            for bit in range(2):
                serves = (target == sub) & (second == bit)
                column = jnp.sum(jnp.where(serves, named, 0.0), axis=1, keepdims=True)
                table = jnp.where(side_lane == LOADS + 2 * step + bit, column, table)
        sides[iter_count - 1] = table

    @pl.loop(0, iter_count)
    def one_pass(t):
        state32 = state[...]
        scale = lax.rsqrt(jnp.mean(state32 * state32, axis=1, keepdims=True) + 1e-06)
        normed = (state32 * scale * gain[...].reshape(1, width).astype(jnp.float32)).astype(jnp.bfloat16)
        rows = rows_all.at[t]
        rows[z, :, :width] = normed
        rows[z, :, width:] = sides[t].astype(jnp.bfloat16)

        @pl.when(t == 0)
        def _():
            pl.semaphore_wait(barrier, 5)

        sent = []

        def share(src, dst, peer, blocks=1):
            k = len(sent)
            sent.append(
                send(
                    rows.at[pl.ds(src, blocks)], rows.at[pl.ds(dst, blocks)],
                    gather_send.at[t, k], gather_recv.at[t, dst], peer,
                )
            )

        def landed(at, blocks=1):
            arrived(rows.at[pl.ds(at, blocks)], gather_send.at[t, 0], gather_recv.at[t, at])

        share(z, CHIPS_Z + z, across)
        for peer in along:
            share(z, z, peer)
        pl.when(t == 0)(count_pairs)
        for at_z in other_z:
            landed(at_z)
            share(at_z, CHIPS_Z + at_z, across)
        share(0, half, sibling, CHIPS_Z)
        for at_z in (z, *other_z):
            landed(CHIPS_Z + at_z)
        share(CHIPS_Z, half + CHIPS_Z, sibling, CHIPS_Z)

        @pl.when(t == 0)
        def _():
            weights[0].wait()
            weights[1].wait()

        for dy in range(CHIPS_Y):
            landed(half + dy * CHIPS_Z, CHIPS_Z)

        def flat_rows():
            return rows[:, :, :width].reshape(all_rows, width)

        @pl.loop(0, hidden_width // TILE)
        def _(i):
            at = pl.ds(pl.multiple_of(i * TILE, TILE), TILE)
            x = flat_rows()
            gate_val = jnp.dot(x, w_gate[:, at], preferred_element_type=jnp.float32)
            up_val = jnp.dot(x, w_up[:, at], preferred_element_type=jnp.float32)
            silu = gate_val / (1.0 + jnp.exp(-gate_val))
            hidden[:, at] = (silu * up_val).astype(jnp.bfloat16)

        side = rows[:, :, width:].reshape(all_rows, LANES).astype(jnp.float32)
        logits = lax.dot_general(
            flat_rows(), router[...], (((1,), (1,)), ((), ())), preferred_element_type=jnp.float32
        )
        sigma = side[:, :FUSED_DEVICES] / (1.0 + jnp.exp(-logits))
        gates = sigma / jnp.sum(sigma, axis=1, keepdims=True)
        gate_lane = lax.broadcasted_iota(jnp.int32, gates.shape, 1)
        gate_col[...] = side[:, FLAG : FLAG + 1] * jnp.sum(
            jnp.where(gate_lane == me, gates, 0.0), axis=1, keepdims=True
        )

        @pl.when(t == iter_count - 1)
        def _():
            total = jnp.sum(rows[:, :, width:].astype(jnp.float32), axis=0)
            row_at = lax.broadcasted_iota(jnp.int32, total.shape, 0)
            own = jnp.sum(jnp.where(row_at == me, total, 0.0), axis=0, keepdims=True)
            load[...] = own[:, LOADS : LOADS + 2 * iter_count] / float(row_count * top_count)

        @pl.when(t == 0)
        def _():
            weights[2].wait()

        def to_core(c):
            return send(
                part.at[t, c, pl.ds(half, half)], from_core.at[t, c], core_send.at[t, c], core_recv.at[t, c], sibling
            )

        def to_y(c):
            arrived(from_core.at[t, c], core_send.at[t, c], core_recv.at[t, c])
            for_y[t, c] = (
                part[t, c, pl.ds(CHIPS_Z, CHIPS_Z)].astype(jnp.float32)
                + from_core[t, c, pl.ds(CHIPS_Z, CHIPS_Z)].astype(jnp.float32)
            ).astype(jnp.bfloat16)
            return send(for_y.at[t, c], from_y.at[t, c], y_send.at[t, c], y_recv.at[t, c], across)

        def summed(c, at_z):
            return (
                part[t, c, at_z].astype(jnp.float32)
                + from_core[t, c, at_z].astype(jnp.float32)
                + from_y[t, c, at_z].astype(jnp.float32)
            )

        def to_z(c):
            arrived(from_y.at[t, c], y_send.at[t, c], y_recv.at[t, c])
            copies = []
            for i in (1, 2, 0):
                for_z[t, c, i] = summed(c, other_z[i]).astype(jnp.bfloat16)
                copies.append(
                    send(
                        for_z.at[t, c, i], from_z.at[t, c, i],
                        z_send.at[t, c, i], z_recv.at[t, c, i], along[i],
                    )
                )
            return copies

        def finish(c):
            total = summed(c, z)
            for i in range(CHIPS_Z - 1):
                arrived(from_z.at[t, c, i], z_send.at[t, c, i], z_recv.at[t, c, i])
                total = total + from_z[t, c, i].astype(jnp.float32)
            at = slice(c * chunk, (c + 1) * chunk)
            state[:, at] = (state[:, at] + total).astype(jnp.bfloat16).astype(jnp.float32)

        for c in range(CHUNKS):
            outs = jnp.dot(
                hidden[...], w_down[:, c * chunk : (c + 1) * chunk],
                preferred_element_type=jnp.float32,
            )
            outs = outs.astype(jnp.bfloat16).astype(jnp.float32) * gate_col[...]
            outs = outs.astype(jnp.bfloat16).reshape(FUSED_DEVICES, row_count, chunk)
            part[t, c] = outs
            sent.append(to_core(c))
            if c >= 1:
                sent.append(to_y(c - 1))
        sent.append(to_y(CHUNKS - 1))
        for c in range(CHUNKS):
            sent.extend(to_z(c))
        for c in range(CHUNKS):
            finish(c)
        for copy in sent:
            copy.wait_send()

    out[...] = state[...].astype(jnp.bfloat16)


def fused_body(
    tokens, depths, routes, norm_gain, router, w_gate, w_up, w_down, replica_plan, copy_choice
):
    row_count, width = tokens.shape
    iter_count = routes.shape[0]
    hidden_width = w_gate.shape[2]
    all_rows = FUSED_DEVICES * row_count
    chunk = width // CHUNKS
    bf16, f32 = jnp.bfloat16, jnp.float32
    dma = pltpu.SemaphoreType.DMA
    vmem = pl.BlockSpec(memory_space=pltpu.VMEM)
    hbm = pl.BlockSpec(memory_space=pltpu.HBM)
    per_chunk = (iter_count, CHUNKS)
    small = (
        tokens, depths.reshape(1, -1), jnp.transpose(routes, (0, 2, 1)), norm_gain,
        replica_plan.reshape(1, -1), copy_choice, jnp.transpose(router),
    )
    return pl.pallas_call(
        fused_kernel,
        out_shape=(
            jax.ShapeDtypeStruct(tokens.shape, bf16),
            jax.ShapeDtypeStruct((1, 2 * iter_count), f32),
        ),
        in_specs=[hbm] * 10,
        out_specs=(vmem, vmem),
        scratch_shapes=[pltpu.VMEM(array.shape, array.dtype) for array in small]
        + [
            pltpu.VMEM((width, hidden_width), bf16),
            pltpu.VMEM((width, hidden_width), bf16),
            pltpu.VMEM((hidden_width, width), bf16),
            pltpu.VMEM((row_count, width), f32),
            pltpu.VMEM((iter_count, row_count, LANES), f32),
            pltpu.VMEM((iter_count, row_count, LANES), f32),
            pltpu.VMEM((iter_count, FUSED_DEVICES, row_count, width + LANES), bf16),
            pltpu.VMEM((all_rows, hidden_width), bf16),
            pltpu.VMEM((all_rows, 1), f32),
            pltpu.VMEM((*per_chunk, FUSED_DEVICES, row_count, chunk), bf16),
            pltpu.VMEM((*per_chunk, CHIPS_Y * CHIPS_Z, row_count, chunk), bf16),
            pltpu.VMEM((*per_chunk, CHIPS_Z, row_count, chunk), bf16),
            pltpu.VMEM((*per_chunk, CHIPS_Z, row_count, chunk), bf16),
            pltpu.VMEM((*per_chunk, CHIPS_Z - 1, row_count, chunk), bf16),
            pltpu.VMEM((*per_chunk, CHIPS_Z - 1, row_count, chunk), bf16),
            dma((len(small),)),
            dma((3,)),
            dma((iter_count, FUSED_DEVICES)),
            dma((iter_count, FUSED_DEVICES)),
            dma(per_chunk),
            dma(per_chunk),
            dma(per_chunk),
            dma(per_chunk),
            dma((*per_chunk, CHIPS_Z - 1)),
            dma((*per_chunk, CHIPS_Z - 1)),
        ],
        compiler_params=pltpu.CompilerParams(
            collective_id=0, has_side_effects=True, vmem_limit_bytes=56 * 1024 * 1024
        ),
        cost_estimate=pl.CostEstimate(
            flops=6 * iter_count * all_rows * width * hidden_width,
            bytes_accessed=6 * width * hidden_width,
            transcendentals=iter_count * all_rows * hidden_width,
        ),
    )(
        *small, w_gate, w_up, w_down,
    )


def expert_ffn(rows_in, gate_w, up_w, down_w):
    gate_val = jnp.dot(rows_in, gate_w, preferred_element_type=jnp.float32)
    up_val = jnp.dot(rows_in, up_w, preferred_element_type=jnp.float32)
    hidden = (jax.nn.silu(gate_val) * up_val).astype(jnp.bfloat16)
    return jnp.dot(hidden, down_w, preferred_element_type=jnp.float32).astype(jnp.bfloat16)


def dispatch_body(
    tokens, depths, routes, norm_gain, router, w_gate, w_up, w_down, replica_plan, copy_choice
):
    highest = lax.Precision.HIGHEST
    peer_count = lax.axis_size("expert")
    row_count, model_width = tokens.shape
    iter_count, _, top_count = routes.shape
    cap_rows = 2 * row_count * top_count // peer_count
    expert_ids = jnp.arange(peer_count, dtype=jnp.int32)
    copy_row = copy_choice[0]
    home_gate, home_up, home_down = (w_gate[0], w_up[0], w_down[0])
    onehot_all = routes[:, :, :, None] == expert_ids
    wanted_all = jnp.sum(jnp.where(onehot_all, copy_row, 0), axis=3)
    plan_at = jnp.sum(jnp.where(wanted_all[..., None] == expert_ids, replica_plan, 0), axis=3)
    valid_all = (plan_at == routes) & (wanted_all != routes)
    target_all = jnp.where(valid_all, wanted_all, routes)
    slot_all = valid_all.astype(jnp.int32)
    active_all = depths[None, :] > jnp.arange(iter_count, dtype=jnp.int32)[:, None]
    live_all = jnp.broadcast_to(active_all[:, :, None], routes.shape)
    bucket_all = target_all * 2 + slot_all
    bucket_hot = (bucket_all[..., None] == jnp.arange(2 * peer_count, dtype=jnp.int32)) & live_all[
        ..., None
    ]
    counts = jnp.sum(bucket_hot.astype(jnp.float32), axis=(1, 2)).reshape(iter_count, peer_count, 2)
    counts = jnp.transpose(counts, (1, 0, 2)).reshape(peer_count, 2 * iter_count)
    copy_load = lax.psum_scatter(counts, "expert", scatter_dimension=0, tiled=True) / float(
        row_count * top_count
    )
    slot_count = 1
    pair_rows = jnp.repeat(jnp.arange(row_count, dtype=jnp.int32), top_count)
    buffer_rows = peer_count * cap_rows * slot_count
    state = tokens
    for layer_step in range(iter_count):
        state32 = state.astype(jnp.float32)
        scale = lax.rsqrt(jnp.mean(state32 * state32, axis=1, keepdims=True) + 1e-06)
        normed = (state32 * scale * norm_gain.astype(jnp.float32)).astype(jnp.bfloat16)
        logits = jnp.dot(normed, router, preferred_element_type=jnp.float32)
        picked = jnp.sum(jnp.where(onehot_all[layer_step], logits[:, None, :], 0.0), axis=2)
        sigmas = jax.nn.sigmoid(picked)
        gates = sigmas / jnp.sum(sigmas, axis=1, keepdims=True)
        target_dev = routes[layer_step]
        live_pairs = live_all[layer_step].reshape(-1)
        bucket = (target_dev * slot_count).reshape(-1)
        bucket_flags = (
            (bucket[:, None] == jnp.arange(peer_count * slot_count, dtype=jnp.int32))
            & live_pairs[:, None]
        ).astype(jnp.int32)
        rank_table = jnp.cumsum(bucket_flags, axis=0)
        position = jnp.sum(rank_table * bucket_flags, axis=1) - 1
        index_flat = (target_dev.reshape(-1) * cap_rows + position) * slot_count
        send_index = jnp.where(live_pairs, index_flat, buffer_rows)
        outbound = (
            jnp.zeros((buffer_rows, model_width), jnp.bfloat16)
            .at[send_index]
            .set(normed[pair_rows], mode="drop")
        )
        outbound = outbound.reshape(peer_count, cap_rows, slot_count, model_width)
        received = lax.all_to_all(outbound, "expert", split_axis=0, concat_axis=0, tiled=True)
        count = received.shape[1]
        first_rows = received[:, :, 0, :].reshape(peer_count * count, model_width)
        result = expert_ffn(first_rows, home_gate, home_up, home_down).reshape(
            peer_count, count, 1, model_width
        )
        returned = lax.all_to_all(result, "expert", split_axis=0, concat_axis=0, tiled=True)
        read_index = jnp.where(live_pairs, index_flat, 0)
        pair_out = returned.reshape(buffer_rows, model_width)[read_index].reshape(
            row_count, top_count, model_width
        )
        weights = gates * live_all[layer_step].astype(jnp.float32)
        delta = jnp.einsum("rk,rkd->rd", weights, pair_out.astype(jnp.float32), precision=highest)
        state = (state32 + delta).astype(jnp.bfloat16)
    return (state, copy_load)


def solution(mesh):
    body = fused_body if mesh.shape["expert"] == FUSED_DEVICES else dispatch_body
    return jax.shard_map(
        body,
        mesh=mesh,
        in_specs=(
            P(("groups", "expert"), None),
            P(("groups", "expert")),
            P(None, ("groups", "expert"), None),
            P(),
            P(),
            P("expert", None, None),
            P("expert", None, None),
            P("expert", None, None),
            P(),
            P("expert", None),
        ),
        out_specs=(P(("groups", "expert"), None), P(("groups", "expert"), None)),
        check_vma=False,
    )
```

```python
import jax
import jax.numpy as jnp
from jax import lax
from jax.experimental import pallas as pl
from jax.experimental.pallas import tpu as pltpu
from jax.sharding import PartitionSpec as P

LANES = 128
FLAG = 32
LOADS = 48
CORES, CHIPS_Y, CHIPS_Z = 2, 2, 4
FUSED_DEVICES = CORES * CHIPS_Y * CHIPS_Z
CHUNKS = 8
TILE = 256


def fused_kernel(
    tokens_hbm, depths_hbm, routes_hbm, gain_hbm, plan_hbm, choice_hbm, router_hbm,
    gate_hbm, up_hbm, down_hbm,
    out, load,
    tokens, depths, routes, gain, plan, choice, router, w_gate, w_up, w_down,
    state, sides, masks, rows_all, hidden, gate_col,
    part, from_core, for_y, from_y, for_z, from_z,
    small_sem, weight_sem, gather_send, gather_recv, core_send, core_recv, y_send, y_recv, z_send, z_recv,
):
    me = lax.axis_index("expert")
    core = me % CORES
    y = (me // CORES) % CHIPS_Y
    z = me // (CORES * CHIPS_Y)
    other_core, other_y = 1 - core, 1 - y
    other_z = (z + 1 - 2 * (z % 2), (z + 2) % CHIPS_Z, CHIPS_Z - 1 - z)

    def device(at_z, at_y, at_core):
        return {"expert": (at_z * CHIPS_Y + at_y) * CORES + at_core}

    sibling = device(z, y, other_core)
    across = device(z, other_y, core)
    along = [device(at, y, core) for at in other_z]

    iter_count, top_count, row_count = routes.shape
    width = tokens.shape[1]
    hidden_width = w_gate.shape[1]
    all_rows = FUSED_DEVICES * row_count
    chunk = width // CHUNKS
    half = CHIPS_Y * CHIPS_Z

    small = [
        pltpu.make_async_copy(src, dst, small_sem.at[i])
        for i, (src, dst) in enumerate(
            (
                (tokens_hbm, tokens), (depths_hbm, depths), (routes_hbm, routes), (gain_hbm, gain),
                (plan_hbm, plan), (choice_hbm, choice), (router_hbm, router),
            )
        )
    ]
    for copy in small:
        copy.start()
    weights = [
        pltpu.make_async_copy(src.at[0], dst, weight_sem.at[i])
        for i, (src, dst) in enumerate(((gate_hbm, w_gate), (up_hbm, w_up), (down_hbm, w_down)))
    ]
    for copy in weights:
        copy.start()

    barrier = pltpu.get_barrier_semaphore()
    for peer in (sibling, across, *along):
        pl.semaphore_signal(barrier, inc=1, device_id=peer, device_id_type=pl.DeviceIdType.MESH)

    def send(src, dst, send_sem, recv_sem, peer):
        copy = pltpu.make_async_remote_copy(
            src_ref=src, dst_ref=dst, send_sem=send_sem, recv_sem=recv_sem,
            device_id=peer, device_id_type=pl.DeviceIdType.MESH,
        )
        copy.start()
        return copy

    def arrived(dst, send_sem, recv_sem):
        pltpu.make_async_remote_copy(
            src_ref=dst, dst_ref=dst, send_sem=send_sem, recv_sem=recv_sem,
            device_id=sibling, device_id_type=pl.DeviceIdType.MESH,
        ).wait_recv()

    for copy in small:
        copy.wait()
    square = (FUSED_DEVICES, FUSED_DEVICES)
    sub = lax.broadcasted_iota(jnp.int32, square, 0)
    lane = lax.broadcasted_iota(jnp.int32, square, 1)
    side_lane = lax.broadcasted_iota(jnp.int32, (row_count, LANES), 1)
    side_sub = lax.broadcasted_iota(jnp.int32, (row_count, LANES), 0)
    diagonal = jnp.where(side_lane == side_sub, 1.0, 0.0).astype(jnp.bfloat16)
    depth_col = jnp.sum(jnp.where(sub == lane, depths[...], 0), axis=1, keepdims=True)
    state[...] = tokens[...].astype(jnp.float32)

    for step in range(iter_count):
        chosen = routes[step]
        hit = sub == chosen[0:1]
        for k in range(1, top_count):
            hit = hit | (sub == chosen[k : k + 1])
        masks[step] = lax.dot_general(
            jnp.where(hit, 1.0, 0.0).astype(jnp.bfloat16), diagonal,
            (((0,), (0,)), ((), ())), preferred_element_type=jnp.float32,
        )
        active = depth_col > step
        sides[step] = jnp.where((side_lane == FLAG) & active, 1.0, masks[step])

    def count_pairs():
        copy_of = choice[...]
        plan_col = jnp.sum(jnp.where(sub == lane, plan[...], 0), axis=1, keepdims=True)
        plan_at = jnp.sum(jnp.where(copy_of == sub, plan_col, 0), axis=0, keepdims=True)
        expert_row = lane[0:1]
        valid = (plan_at == expert_row) & (copy_of != expert_row)
        target = jnp.where(valid, copy_of, expert_row)
        second = valid.astype(jnp.int32)
        table = sides[iter_count - 1]
        for step in range(iter_count):
            live = jnp.where(depth_col > step, masks[step], 0.0)
            named = jnp.sum(live, axis=0, keepdims=True)[:, :FUSED_DEVICES]
            for bit in range(2):
                serves = (target == sub) & (second == bit)
                column = jnp.sum(jnp.where(serves, named, 0.0), axis=1, keepdims=True)
                table = jnp.where(side_lane == LOADS + 2 * step + bit, column, table)
        sides[iter_count - 1] = table

    @pl.loop(0, iter_count)
    def one_pass(t):
        state32 = state[...]
        scale = lax.rsqrt(jnp.mean(state32 * state32, axis=1, keepdims=True) + 1e-06)
        normed = (state32 * scale * gain[...].reshape(1, width).astype(jnp.float32)).astype(jnp.bfloat16)
        rows = rows_all.at[t]
        rows[z, :, :width] = normed
        rows[z, :, width:] = sides[t].astype(jnp.bfloat16)

        @pl.when(t == 0)
        def _():
            pl.semaphore_wait(barrier, 5)

        sent = []

        def share(src, dst, peer, blocks=1):
            k = len(sent)
            sent.append(
                send(
                    rows.at[pl.ds(src, blocks)], rows.at[pl.ds(dst, blocks)],
                    gather_send.at[t, k], gather_recv.at[t, dst], peer,
                )
            )

        def landed(at, blocks=1):
            arrived(rows.at[pl.ds(at, blocks)], gather_send.at[t, 0], gather_recv.at[t, at])

        share(z, CHIPS_Z + z, across)
        for peer in along:
            share(z, z, peer)
        pl.when(t == 0)(count_pairs)
        for at_z in other_z:
            landed(at_z)
            share(at_z, CHIPS_Z + at_z, across)
        share(0, half, sibling, CHIPS_Z)
        for at_z in (z, *other_z):
            landed(CHIPS_Z + at_z)
        share(CHIPS_Z, half + CHIPS_Z, sibling, CHIPS_Z)

        @pl.when(t == 0)
        def _():
            weights[0].wait()
            weights[1].wait()

        for dy in range(CHIPS_Y):
            landed(half + dy * CHIPS_Z, CHIPS_Z)

        def flat_rows():
            return rows[:, :, :width].reshape(all_rows, width)

        @pl.loop(0, hidden_width // TILE)
        def _(i):
            at = pl.ds(pl.multiple_of(i * TILE, TILE), TILE)
            x = flat_rows()
            gate_val = jnp.dot(x, w_gate[:, at], preferred_element_type=jnp.float32)
            up_val = jnp.dot(x, w_up[:, at], preferred_element_type=jnp.float32)
            silu = gate_val / (1.0 + jnp.exp(-gate_val))
            hidden[:, at] = (silu * up_val).astype(jnp.bfloat16)

        side = rows[:, :, width:].reshape(all_rows, LANES).astype(jnp.float32)
        logits = lax.dot_general(
            flat_rows(), router[...], (((1,), (1,)), ((), ())), preferred_element_type=jnp.float32
        )
        sigma = side[:, :FUSED_DEVICES] / (1.0 + jnp.exp(-logits))
        gates = sigma / jnp.sum(sigma, axis=1, keepdims=True)
        gate_lane = lax.broadcasted_iota(jnp.int32, gates.shape, 1)
        gate_col[...] = side[:, FLAG : FLAG + 1] * jnp.sum(
            jnp.where(gate_lane == me, gates, 0.0), axis=1, keepdims=True
        )

        @pl.when(t == iter_count - 1)
        def _():
            total = jnp.sum(rows[:, :, width:].astype(jnp.float32), axis=0)
            row_at = lax.broadcasted_iota(jnp.int32, total.shape, 0)
            own = jnp.sum(jnp.where(row_at == me, total, 0.0), axis=0, keepdims=True)
            load[...] = own[:, LOADS : LOADS + 2 * iter_count] / float(row_count * top_count)

        @pl.when(t == 0)
        def _():
            weights[2].wait()

        def to_core(c):
            return send(
                part.at[t, c, pl.ds(half, half)], from_core.at[t, c], core_send.at[t, c], core_recv.at[t, c], sibling
            )

        def to_y(c):
            arrived(from_core.at[t, c], core_send.at[t, c], core_recv.at[t, c])
            for_y[t, c] = (
                part[t, c, pl.ds(CHIPS_Z, CHIPS_Z)].astype(jnp.float32)
                + from_core[t, c, pl.ds(CHIPS_Z, CHIPS_Z)].astype(jnp.float32)
            ).astype(jnp.bfloat16)
            return send(for_y.at[t, c], from_y.at[t, c], y_send.at[t, c], y_recv.at[t, c], across)

        def summed(c, at_z):
            return (
                part[t, c, at_z].astype(jnp.float32)
                + from_core[t, c, at_z].astype(jnp.float32)
                + from_y[t, c, at_z].astype(jnp.float32)
            )

        def to_z(c):
            arrived(from_y.at[t, c], y_send.at[t, c], y_recv.at[t, c])
            copies = []
            for i in (1, 2, 0):
                for_z[t, c, i] = summed(c, other_z[i]).astype(jnp.bfloat16)
                copies.append(
                    send(
                        for_z.at[t, c, i], from_z.at[t, c, i],
                        z_send.at[t, c, i], z_recv.at[t, c, i], along[i],
                    )
                )
            return copies

        def finish(c):
            total = summed(c, z)
            for i in range(CHIPS_Z - 1):
                arrived(from_z.at[t, c, i], z_send.at[t, c, i], z_recv.at[t, c, i])
                total = total + from_z[t, c, i].astype(jnp.float32)
            at = slice(c * chunk, (c + 1) * chunk)
            state[:, at] = (state[:, at] + total).astype(jnp.bfloat16).astype(jnp.float32)

        for c in range(CHUNKS):
            outs = jnp.dot(
                hidden[...], w_down[:, c * chunk : (c + 1) * chunk],
                preferred_element_type=jnp.float32,
            )
            outs = outs.astype(jnp.bfloat16).astype(jnp.float32) * gate_col[...]
            outs = outs.astype(jnp.bfloat16).reshape(FUSED_DEVICES, row_count, chunk)
            part[t, c] = outs
            sent.append(to_core(c))
            if c >= 1:
                sent.append(to_y(c - 1))
        sent.append(to_y(CHUNKS - 1))
        for c in range(CHUNKS):
            sent.extend(to_z(c))
        for c in range(CHUNKS):
            finish(c)
        for copy in sent:
            copy.wait_send()

    out[...] = state[...].astype(jnp.bfloat16)


def fused_body(
    tokens, depths, routes, norm_gain, router, w_gate, w_up, w_down, replica_plan, copy_choice
):
    row_count, width = tokens.shape
    iter_count = routes.shape[0]
    hidden_width = w_gate.shape[2]
    all_rows = FUSED_DEVICES * row_count
    chunk = width // CHUNKS
    bf16, f32 = jnp.bfloat16, jnp.float32
    dma = pltpu.SemaphoreType.DMA
    vmem = pl.BlockSpec(memory_space=pltpu.VMEM)
    hbm = pl.BlockSpec(memory_space=pltpu.HBM)
    per_chunk = (iter_count, CHUNKS)
    small = (
        tokens, depths.reshape(1, -1), jnp.transpose(routes, (0, 2, 1)), norm_gain,
        replica_plan.reshape(1, -1), copy_choice, jnp.transpose(router),
    )
    return pl.pallas_call(
        fused_kernel,
        out_shape=(
            jax.ShapeDtypeStruct(tokens.shape, bf16),
            jax.ShapeDtypeStruct((1, 2 * iter_count), f32),
        ),
        in_specs=[hbm] * 10,
        out_specs=(vmem, vmem),
        scratch_shapes=[pltpu.VMEM(array.shape, array.dtype) for array in small]
        + [
            pltpu.VMEM((width, hidden_width), bf16),
            pltpu.VMEM((width, hidden_width), bf16),
            pltpu.VMEM((hidden_width, width), bf16),
            pltpu.VMEM((row_count, width), f32),
            pltpu.VMEM((iter_count, row_count, LANES), f32),
            pltpu.VMEM((iter_count, row_count, LANES), f32),
            pltpu.VMEM((iter_count, FUSED_DEVICES, row_count, width + LANES), bf16),
            pltpu.VMEM((all_rows, hidden_width), bf16),
            pltpu.VMEM((all_rows, 1), f32),
            pltpu.VMEM((*per_chunk, FUSED_DEVICES, row_count, chunk), bf16),
            pltpu.VMEM((*per_chunk, CHIPS_Y * CHIPS_Z, row_count, chunk), bf16),
            pltpu.VMEM((*per_chunk, CHIPS_Z, row_count, chunk), bf16),
            pltpu.VMEM((*per_chunk, CHIPS_Z, row_count, chunk), bf16),
            pltpu.VMEM((*per_chunk, CHIPS_Z - 1, row_count, chunk), bf16),
            pltpu.VMEM((*per_chunk, CHIPS_Z - 1, row_count, chunk), bf16),
            dma((len(small),)),
            dma((3,)),
            dma((iter_count, FUSED_DEVICES)),
            dma((iter_count, FUSED_DEVICES)),
            dma(per_chunk),
            dma(per_chunk),
            dma(per_chunk),
            dma(per_chunk),
            dma((*per_chunk, CHIPS_Z - 1)),
            dma((*per_chunk, CHIPS_Z - 1)),
        ],
        compiler_params=pltpu.CompilerParams(
            collective_id=0, has_side_effects=True, vmem_limit_bytes=56 * 1024 * 1024
        ),
        cost_estimate=pl.CostEstimate(
            flops=6 * iter_count * all_rows * width * hidden_width,
            bytes_accessed=6 * width * hidden_width,
            transcendentals=iter_count * all_rows * hidden_width,
        ),
    )(
        *small, w_gate, w_up, w_down,
    )


def expert_ffn(rows_in, gate_w, up_w, down_w):
    gate_val = jnp.dot(rows_in, gate_w, preferred_element_type=jnp.float32)
    up_val = jnp.dot(rows_in, up_w, preferred_element_type=jnp.float32)
    hidden = (jax.nn.silu(gate_val) * up_val).astype(jnp.bfloat16)
    return jnp.dot(hidden, down_w, preferred_element_type=jnp.float32).astype(jnp.bfloat16)


def dispatch_body(
    tokens, depths, routes, norm_gain, router, w_gate, w_up, w_down, replica_plan, copy_choice
):
    highest = lax.Precision.HIGHEST
    peer_count = lax.axis_size("expert")
    row_count, model_width = tokens.shape
    iter_count, _, top_count = routes.shape
    cap_rows = 2 * row_count * top_count // peer_count
    expert_ids = jnp.arange(peer_count, dtype=jnp.int32)
    copy_row = copy_choice[0]
    home_gate, home_up, home_down = (w_gate[0], w_up[0], w_down[0])
    onehot_all = routes[:, :, :, None] == expert_ids
    wanted_all = jnp.sum(jnp.where(onehot_all, copy_row, 0), axis=3)
    plan_at = jnp.sum(jnp.where(wanted_all[..., None] == expert_ids, replica_plan, 0), axis=3)
    valid_all = (plan_at == routes) & (wanted_all != routes)
    target_all = jnp.where(valid_all, wanted_all, routes)
    slot_all = valid_all.astype(jnp.int32)
    active_all = depths[None, :] > jnp.arange(iter_count, dtype=jnp.int32)[:, None]
    live_all = jnp.broadcast_to(active_all[:, :, None], routes.shape)
    bucket_all = target_all * 2 + slot_all
    bucket_hot = (bucket_all[..., None] == jnp.arange(2 * peer_count, dtype=jnp.int32)) & live_all[
        ..., None
    ]
    counts = jnp.sum(bucket_hot.astype(jnp.float32), axis=(1, 2)).reshape(iter_count, peer_count, 2)
    counts = jnp.transpose(counts, (1, 0, 2)).reshape(peer_count, 2 * iter_count)
    copy_load = lax.psum_scatter(counts, "expert", scatter_dimension=0, tiled=True) / float(
        row_count * top_count
    )
    slot_count = 1
    pair_rows = jnp.repeat(jnp.arange(row_count, dtype=jnp.int32), top_count)
    buffer_rows = peer_count * cap_rows * slot_count
    state = tokens
    for layer_step in range(iter_count):
        state32 = state.astype(jnp.float32)
        scale = lax.rsqrt(jnp.mean(state32 * state32, axis=1, keepdims=True) + 1e-06)
        normed = (state32 * scale * norm_gain.astype(jnp.float32)).astype(jnp.bfloat16)
        logits = jnp.dot(normed, router, preferred_element_type=jnp.float32)
        picked = jnp.sum(jnp.where(onehot_all[layer_step], logits[:, None, :], 0.0), axis=2)
        sigmas = jax.nn.sigmoid(picked)
        gates = sigmas / jnp.sum(sigmas, axis=1, keepdims=True)
        target_dev = routes[layer_step]
        live_pairs = live_all[layer_step].reshape(-1)
        bucket = (target_dev * slot_count).reshape(-1)
        bucket_flags = (
            (bucket[:, None] == jnp.arange(peer_count * slot_count, dtype=jnp.int32))
            & live_pairs[:, None]
        ).astype(jnp.int32)
        rank_table = jnp.cumsum(bucket_flags, axis=0)
        position = jnp.sum(rank_table * bucket_flags, axis=1) - 1
        index_flat = (target_dev.reshape(-1) * cap_rows + position) * slot_count
        send_index = jnp.where(live_pairs, index_flat, buffer_rows)
        outbound = (
            jnp.zeros((buffer_rows, model_width), jnp.bfloat16)
            .at[send_index]
            .set(normed[pair_rows], mode="drop")
        )
        outbound = outbound.reshape(peer_count, cap_rows, slot_count, model_width)
        received = lax.all_to_all(outbound, "expert", split_axis=0, concat_axis=0, tiled=True)
        count = received.shape[1]
        first_rows = received[:, :, 0, :].reshape(peer_count * count, model_width)
        result = expert_ffn(first_rows, home_gate, home_up, home_down).reshape(
            peer_count, count, 1, model_width
        )
        returned = lax.all_to_all(result, "expert", split_axis=0, concat_axis=0, tiled=True)
        read_index = jnp.where(live_pairs, index_flat, 0)
        pair_out = returned.reshape(buffer_rows, model_width)[read_index].reshape(
            row_count, top_count, model_width
        )
        weights = gates * live_all[layer_step].astype(jnp.float32)
        delta = jnp.einsum("rk,rkd->rd", weights, pair_out.astype(jnp.float32), precision=highest)
        state = (state32 + delta).astype(jnp.bfloat16)
    return (state, copy_load)


def solution(mesh):
    body = fused_body if mesh.shape["expert"] == FUSED_DEVICES else dispatch_body
    return jax.shard_map(
        body,
        mesh=mesh,
        in_specs=(
            P(("groups", "expert"), None),
            P(("groups", "expert")),
            P(None, ("groups", "expert"), None),
            P(),
            P(),
            P("expert", None, None),
            P("expert", None, None),
            P("expert", None, None),
            P(),
            P("expert", None),
        ),
        out_specs=(P(("groups", "expert"), None), P(("groups", "expert"), None)),
        check_vma=False,
    )
```

```python
import jax
import jax.numpy as jnp
from jax import lax
from jax.experimental import pallas as pl
from jax.experimental.pallas import tpu as pltpu
from jax.sharding import PartitionSpec as P

LANES = 128
FLAG = 32
LOADS = 48
CORES, CHIPS_Y, CHIPS_Z = 2, 2, 4
FUSED_DEVICES = CORES * CHIPS_Y * CHIPS_Z
CHUNKS = 4
TILE = 256


def fused_kernel(
    tokens_hbm, depths_hbm, routes_hbm, gain_hbm, plan_hbm, choice_hbm, router_hbm,
    gate_hbm, up_hbm, down_hbm,
    out, load,
    tokens, depths, routes, gain, plan, choice, router, w_gate, w_up, w_down,
    state, sides, masks, rows_all, hidden, gate_col,
    part, from_core, for_y, from_y, for_z, from_z,
    small_sem, weight_sem, gather_send, gather_recv, core_send, core_recv, y_send, y_recv, z_send, z_recv,
):
    me = lax.axis_index("expert")
    core = me % CORES
    y = (me // CORES) % CHIPS_Y
    z = me // (CORES * CHIPS_Y)
    other_core, other_y = 1 - core, 1 - y
    other_z = (z + 1 - 2 * (z % 2), (z + 2) % CHIPS_Z, CHIPS_Z - 1 - z)

    def device(at_z, at_y, at_core):
        return {"expert": (at_z * CHIPS_Y + at_y) * CORES + at_core}

    sibling = device(z, y, other_core)
    across = device(z, other_y, core)
    along = [device(at, y, core) for at in other_z]

    iter_count, top_count, row_count = routes.shape
    width = tokens.shape[1]
    hidden_width = w_gate.shape[1]
    all_rows = FUSED_DEVICES * row_count
    chunk = width // CHUNKS
    half = CHIPS_Y * CHIPS_Z

    small = [
        pltpu.make_async_copy(src, dst, small_sem.at[i])
        for i, (src, dst) in enumerate(
            (
                (tokens_hbm, tokens), (depths_hbm, depths), (routes_hbm, routes), (gain_hbm, gain),
                (plan_hbm, plan), (choice_hbm, choice), (router_hbm, router),
            )
        )
    ]
    for copy in small:
        copy.start()
    weights = [
        pltpu.make_async_copy(src.at[0], dst, weight_sem.at[i])
        for i, (src, dst) in enumerate(((gate_hbm, w_gate), (up_hbm, w_up), (down_hbm, w_down)))
    ]
    for copy in weights:
        copy.start()

    barrier = pltpu.get_barrier_semaphore()
    for peer in (sibling, across, *along):
        pl.semaphore_signal(barrier, inc=1, device_id=peer, device_id_type=pl.DeviceIdType.MESH)

    def send(src, dst, send_sem, recv_sem, peer):
        copy = pltpu.make_async_remote_copy(
            src_ref=src, dst_ref=dst, send_sem=send_sem, recv_sem=recv_sem,
            device_id=peer, device_id_type=pl.DeviceIdType.MESH,
        )
        copy.start()
        return copy

    def arrived(dst, send_sem, recv_sem):
        pltpu.make_async_remote_copy(
            src_ref=dst, dst_ref=dst, send_sem=send_sem, recv_sem=recv_sem,
            device_id=sibling, device_id_type=pl.DeviceIdType.MESH,
        ).wait_recv()

    for copy in small:
        copy.wait()
    square = (FUSED_DEVICES, FUSED_DEVICES)
    sub = lax.broadcasted_iota(jnp.int32, square, 0)
    lane = lax.broadcasted_iota(jnp.int32, square, 1)
    side_lane = lax.broadcasted_iota(jnp.int32, (row_count, LANES), 1)
    side_sub = lax.broadcasted_iota(jnp.int32, (row_count, LANES), 0)
    diagonal = jnp.where(side_lane == side_sub, 1.0, 0.0).astype(jnp.bfloat16)
    depth_col = jnp.sum(jnp.where(sub == lane, depths[...], 0), axis=1, keepdims=True)
    state[...] = tokens[...].astype(jnp.float32)

    for step in range(iter_count):
        chosen = routes[step]
        hit = sub == chosen[0:1]
        for k in range(1, top_count):
            hit = hit | (sub == chosen[k : k + 1])
        masks[step] = lax.dot_general(
            jnp.where(hit, 1.0, 0.0).astype(jnp.bfloat16), diagonal,
            (((0,), (0,)), ((), ())), preferred_element_type=jnp.float32,
        )
        active = depth_col > step
        sides[step] = jnp.where((side_lane == FLAG) & active, 1.0, masks[step])

    def count_pairs():
        copy_of = choice[...]
        plan_col = jnp.sum(jnp.where(sub == lane, plan[...], 0), axis=1, keepdims=True)
        plan_at = jnp.sum(jnp.where(copy_of == sub, plan_col, 0), axis=0, keepdims=True)
        expert_row = lane[0:1]
        valid = (plan_at == expert_row) & (copy_of != expert_row)
        target = jnp.where(valid, copy_of, expert_row)
        second = valid.astype(jnp.int32)
        table = sides[iter_count - 1]
        for step in range(iter_count):
            live = jnp.where(depth_col > step, masks[step], 0.0)
            named = jnp.sum(live, axis=0, keepdims=True)[:, :FUSED_DEVICES]
            for bit in range(2):
                serves = (target == sub) & (second == bit)
                column = jnp.sum(jnp.where(serves, named, 0.0), axis=1, keepdims=True)
                table = jnp.where(side_lane == LOADS + 2 * step + bit, column, table)
        sides[iter_count - 1] = table

    @pl.loop(0, iter_count)
    def one_pass(t):
        state32 = state[...]
        scale = lax.rsqrt(jnp.mean(state32 * state32, axis=1, keepdims=True) + 1e-06)
        normed = (state32 * scale * gain[...].reshape(1, width).astype(jnp.float32)).astype(jnp.bfloat16)
        rows = rows_all.at[t]
        rows[z, :, :width] = normed
        rows[z, :, width:] = sides[t].astype(jnp.bfloat16)

        @pl.when(t == 0)
        def _():
            pl.semaphore_wait(barrier, 5)

        sent = []

        def share(src, dst, peer, blocks=1):
            k = len(sent)
            sent.append(
                send(
                    rows.at[pl.ds(src, blocks)], rows.at[pl.ds(dst, blocks)],
                    gather_send.at[t, k], gather_recv.at[t, dst], peer,
                )
            )

        def landed(at, blocks=1):
            arrived(rows.at[pl.ds(at, blocks)], gather_send.at[t, 0], gather_recv.at[t, at])

        share(z, CHIPS_Z + z, across)
        for peer in along:
            share(z, z, peer)
        pl.when(t == 0)(count_pairs)
        for at_z in other_z:
            landed(at_z)
            share(at_z, CHIPS_Z + at_z, across)
        share(0, half, sibling, CHIPS_Z)
        for at_z in (z, *other_z):
            landed(CHIPS_Z + at_z)
        share(CHIPS_Z, half + CHIPS_Z, sibling, CHIPS_Z)

        def gates_of(first):
            here = rows[first : first + half]
            side = here[:, :, width:].reshape(all_rows // 2, LANES).astype(jnp.float32)
            logits = lax.dot_general(
                here[:, :, :width].reshape(all_rows // 2, width), router[...],
                (((1,), (1,)), ((), ())), preferred_element_type=jnp.float32,
            )
            sigma = side[:, :FUSED_DEVICES] / (1.0 + jnp.exp(-logits))
            gates = sigma / jnp.sum(sigma, axis=1, keepdims=True)
            gate_lane = lax.broadcasted_iota(jnp.int32, gates.shape, 1)
            span = slice(first * row_count, (first + half) * row_count)
            gate_col[span] = side[:, FLAG : FLAG + 1] * jnp.sum(
                jnp.where(gate_lane == me, gates, 0.0), axis=1, keepdims=True
            )

        gates_of(0)

        @pl.when(t == 0)
        def _():
            weights[0].wait()
            weights[1].wait()

        for dy in range(CHIPS_Y):
            landed(half + dy * CHIPS_Z, CHIPS_Z)

        def flat_rows():
            return rows[:, :, :width].reshape(all_rows, width)

        @pl.loop(0, hidden_width // TILE)
        def _(i):
            at = pl.ds(pl.multiple_of(i * TILE, TILE), TILE)
            x = flat_rows()
            gate_val = jnp.dot(x, w_gate[:, at], preferred_element_type=jnp.float32)
            up_val = jnp.dot(x, w_up[:, at], preferred_element_type=jnp.float32)
            silu = gate_val / (1.0 + jnp.exp(-gate_val))
            hidden[:, at] = (silu * up_val).astype(jnp.bfloat16)

        gates_of(half)

        @pl.when(t == 0)
        def _():
            weights[2].wait()

        def to_core(c):
            return send(
                part.at[t, c, pl.ds(half, half)], from_core.at[t, c], core_send.at[t, c], core_recv.at[t, c], sibling
            )

        def to_y(c):
            arrived(from_core.at[t, c], core_send.at[t, c], core_recv.at[t, c])
            for_y[t, c] = (
                part[t, c, pl.ds(CHIPS_Z, CHIPS_Z)].astype(jnp.float32)
                + from_core[t, c, pl.ds(CHIPS_Z, CHIPS_Z)].astype(jnp.float32)
            ).astype(jnp.bfloat16)
            return send(for_y.at[t, c], from_y.at[t, c], y_send.at[t, c], y_recv.at[t, c], across)

        def summed(c, at_z):
            return (
                part[t, c, at_z].astype(jnp.float32)
                + from_core[t, c, at_z].astype(jnp.float32)
                + from_y[t, c, at_z].astype(jnp.float32)
            )

        def to_z(c):
            arrived(from_y.at[t, c], y_send.at[t, c], y_recv.at[t, c])
            copies = []
            for i in (1, 2, 0):
                for_z[t, c, i] = summed(c, other_z[i]).astype(jnp.bfloat16)
                copies.append(
                    send(
                        for_z.at[t, c, i], from_z.at[t, c, i],
                        z_send.at[t, c, i], z_recv.at[t, c, i], along[i],
                    )
                )
            return copies

        def finish(c):
            total = summed(c, z)
            for i in range(CHIPS_Z - 1):
                arrived(from_z.at[t, c, i], z_send.at[t, c, i], z_recv.at[t, c, i])
                total = total + from_z[t, c, i].astype(jnp.float32)
            at = slice(c * chunk, (c + 1) * chunk)
            state[:, at] = (state[:, at] + total).astype(jnp.bfloat16).astype(jnp.float32)

        for c in range(CHUNKS):
            outs = jnp.dot(
                hidden[...], w_down[:, c * chunk : (c + 1) * chunk],
                preferred_element_type=jnp.float32,
            )
            outs = outs.astype(jnp.bfloat16).astype(jnp.float32) * gate_col[...]
            outs = outs.astype(jnp.bfloat16).reshape(FUSED_DEVICES, row_count, chunk)
            part[t, c] = outs
            sent.append(to_core(c))
            if c >= 1:
                sent.append(to_y(c - 1))
        sent.append(to_y(CHUNKS - 1))

        @pl.when(t == iter_count - 1)
        def _():
            total = jnp.sum(rows[:, :, width:].astype(jnp.float32), axis=0)
            row_at = lax.broadcasted_iota(jnp.int32, total.shape, 0)
            own = jnp.sum(jnp.where(row_at == me, total, 0.0), axis=0, keepdims=True)
            load[...] = own[:, LOADS : LOADS + 2 * iter_count] / float(row_count * top_count)

        for c in range(CHUNKS):
            sent.extend(to_z(c))
        for c in range(CHUNKS):
            finish(c)
        for copy in sent:
            copy.wait_send()

    out[...] = state[...].astype(jnp.bfloat16)


def fused_body(
    tokens, depths, routes, norm_gain, router, w_gate, w_up, w_down, replica_plan, copy_choice
):
    row_count, width = tokens.shape
    iter_count = routes.shape[0]
    hidden_width = w_gate.shape[2]
    all_rows = FUSED_DEVICES * row_count
    chunk = width // CHUNKS
    bf16, f32 = jnp.bfloat16, jnp.float32
    dma = pltpu.SemaphoreType.DMA
    vmem = pl.BlockSpec(memory_space=pltpu.VMEM)
    hbm = pl.BlockSpec(memory_space=pltpu.HBM)
    per_chunk = (iter_count, CHUNKS)
    small = (
        tokens, depths.reshape(1, -1), jnp.transpose(routes, (0, 2, 1)), norm_gain,
        replica_plan.reshape(1, -1), copy_choice, jnp.transpose(router),
    )
    return pl.pallas_call(
        fused_kernel,
        out_shape=(
            jax.ShapeDtypeStruct(tokens.shape, bf16),
            jax.ShapeDtypeStruct((1, 2 * iter_count), f32),
        ),
        in_specs=[hbm] * 10,
        out_specs=(vmem, vmem),
        scratch_shapes=[pltpu.VMEM(array.shape, array.dtype) for array in small]
        + [
            pltpu.VMEM((width, hidden_width), bf16),
            pltpu.VMEM((width, hidden_width), bf16),
            pltpu.VMEM((hidden_width, width), bf16),
            pltpu.VMEM((row_count, width), f32),
            pltpu.VMEM((iter_count, row_count, LANES), f32),
            pltpu.VMEM((iter_count, row_count, LANES), f32),
            pltpu.VMEM((iter_count, FUSED_DEVICES, row_count, width + LANES), bf16),
            pltpu.VMEM((all_rows, hidden_width), bf16),
            pltpu.VMEM((all_rows, 1), f32),
            pltpu.VMEM((*per_chunk, FUSED_DEVICES, row_count, chunk), bf16),
            pltpu.VMEM((*per_chunk, CHIPS_Y * CHIPS_Z, row_count, chunk), bf16),
            pltpu.VMEM((*per_chunk, CHIPS_Z, row_count, chunk), bf16),
            pltpu.VMEM((*per_chunk, CHIPS_Z, row_count, chunk), bf16),
            pltpu.VMEM((*per_chunk, CHIPS_Z - 1, row_count, chunk), bf16),
            pltpu.VMEM((*per_chunk, CHIPS_Z - 1, row_count, chunk), bf16),
            dma((len(small),)),
            dma((3,)),
            dma((iter_count, FUSED_DEVICES)),
            dma((iter_count, FUSED_DEVICES)),
            dma(per_chunk),
            dma(per_chunk),
            dma(per_chunk),
            dma(per_chunk),
            dma((*per_chunk, CHIPS_Z - 1)),
            dma((*per_chunk, CHIPS_Z - 1)),
        ],
        compiler_params=pltpu.CompilerParams(
            collective_id=0, has_side_effects=True, vmem_limit_bytes=56 * 1024 * 1024
        ),
        cost_estimate=pl.CostEstimate(
            flops=6 * iter_count * all_rows * width * hidden_width,
            bytes_accessed=6 * width * hidden_width,
            transcendentals=iter_count * all_rows * hidden_width,
        ),
    )(
        *small, w_gate, w_up, w_down,
    )


def expert_ffn(rows_in, gate_w, up_w, down_w):
    gate_val = jnp.dot(rows_in, gate_w, preferred_element_type=jnp.float32)
    up_val = jnp.dot(rows_in, up_w, preferred_element_type=jnp.float32)
    hidden = (jax.nn.silu(gate_val) * up_val).astype(jnp.bfloat16)
    return jnp.dot(hidden, down_w, preferred_element_type=jnp.float32).astype(jnp.bfloat16)


def dispatch_body(
    tokens, depths, routes, norm_gain, router, w_gate, w_up, w_down, replica_plan, copy_choice
):
    highest = lax.Precision.HIGHEST
    peer_count = lax.axis_size("expert")
    row_count, model_width = tokens.shape
    iter_count, _, top_count = routes.shape
    cap_rows = 2 * row_count * top_count // peer_count
    expert_ids = jnp.arange(peer_count, dtype=jnp.int32)
    copy_row = copy_choice[0]
    home_gate, home_up, home_down = (w_gate[0], w_up[0], w_down[0])
    onehot_all = routes[:, :, :, None] == expert_ids
    wanted_all = jnp.sum(jnp.where(onehot_all, copy_row, 0), axis=3)
    plan_at = jnp.sum(jnp.where(wanted_all[..., None] == expert_ids, replica_plan, 0), axis=3)
    valid_all = (plan_at == routes) & (wanted_all != routes)
    target_all = jnp.where(valid_all, wanted_all, routes)
    slot_all = valid_all.astype(jnp.int32)
    active_all = depths[None, :] > jnp.arange(iter_count, dtype=jnp.int32)[:, None]
    live_all = jnp.broadcast_to(active_all[:, :, None], routes.shape)
    bucket_all = target_all * 2 + slot_all
    bucket_hot = (bucket_all[..., None] == jnp.arange(2 * peer_count, dtype=jnp.int32)) & live_all[
        ..., None
    ]
    counts = jnp.sum(bucket_hot.astype(jnp.float32), axis=(1, 2)).reshape(iter_count, peer_count, 2)
    counts = jnp.transpose(counts, (1, 0, 2)).reshape(peer_count, 2 * iter_count)
    copy_load = lax.psum_scatter(counts, "expert", scatter_dimension=0, tiled=True) / float(
        row_count * top_count
    )
    slot_count = 1
    pair_rows = jnp.repeat(jnp.arange(row_count, dtype=jnp.int32), top_count)
    buffer_rows = peer_count * cap_rows * slot_count
    state = tokens
    for layer_step in range(iter_count):
        state32 = state.astype(jnp.float32)
        scale = lax.rsqrt(jnp.mean(state32 * state32, axis=1, keepdims=True) + 1e-06)
        normed = (state32 * scale * norm_gain.astype(jnp.float32)).astype(jnp.bfloat16)
        logits = jnp.dot(normed, router, preferred_element_type=jnp.float32)
        picked = jnp.sum(jnp.where(onehot_all[layer_step], logits[:, None, :], 0.0), axis=2)
        sigmas = jax.nn.sigmoid(picked)
        gates = sigmas / jnp.sum(sigmas, axis=1, keepdims=True)
        target_dev = routes[layer_step]
        live_pairs = live_all[layer_step].reshape(-1)
        bucket = (target_dev * slot_count).reshape(-1)
        bucket_flags = (
            (bucket[:, None] == jnp.arange(peer_count * slot_count, dtype=jnp.int32))
            & live_pairs[:, None]
        ).astype(jnp.int32)
        rank_table = jnp.cumsum(bucket_flags, axis=0)
        position = jnp.sum(rank_table * bucket_flags, axis=1) - 1
        index_flat = (target_dev.reshape(-1) * cap_rows + position) * slot_count
        send_index = jnp.where(live_pairs, index_flat, buffer_rows)
        outbound = (
            jnp.zeros((buffer_rows, model_width), jnp.bfloat16)
            .at[send_index]
            .set(normed[pair_rows], mode="drop")
        )
        outbound = outbound.reshape(peer_count, cap_rows, slot_count, model_width)
        received = lax.all_to_all(outbound, "expert", split_axis=0, concat_axis=0, tiled=True)
        count = received.shape[1]
        first_rows = received[:, :, 0, :].reshape(peer_count * count, model_width)
        result = expert_ffn(first_rows, home_gate, home_up, home_down).reshape(
            peer_count, count, 1, model_width
        )
        returned = lax.all_to_all(result, "expert", split_axis=0, concat_axis=0, tiled=True)
        read_index = jnp.where(live_pairs, index_flat, 0)
        pair_out = returned.reshape(buffer_rows, model_width)[read_index].reshape(
            row_count, top_count, model_width
        )
        weights = gates * live_all[layer_step].astype(jnp.float32)
        delta = jnp.einsum("rk,rkd->rd", weights, pair_out.astype(jnp.float32), precision=highest)
        state = (state32 + delta).astype(jnp.bfloat16)
    return (state, copy_load)


def solution(mesh):
    body = fused_body if mesh.shape["expert"] == FUSED_DEVICES else dispatch_body
    return jax.shard_map(
        body,
        mesh=mesh,
        in_specs=(
            P(("groups", "expert"), None),
            P(("groups", "expert")),
            P(None, ("groups", "expert"), None),
            P(),
            P(),
            P("expert", None, None),
            P("expert", None, None),
            P("expert", None, None),
            P(),
            P("expert", None),
        ),
        out_specs=(P(("groups", "expert"), None), P(("groups", "expert"), None)),
        check_vma=False,
    )
```
